32 devices in a mesh: node: 4 (over y, core), tm: 8 (over z, x).
Axes of the slice: x: 2, y: 2, z: 4, core: 2. Of those that a mesh axis runs over, the one named last changes fastest.
Arguments:
- memory: bfloat16 [32768, 1024], P(('node', 'tm')), may hold values from -6 to 6
- ends_owner: int32 [8192, 2], P(('node', 'tm')), may hold values from 0 to 31, all different within a row; in each aligned block of 256 rows (0 to 255, 256 to 511, ...) at most 20 rows name the same one
- ends_row: int32 [8192, 2], P(('node', 'tm')), may hold values from 0 to 1023
- event_mask: int32 [8192], P(('node', 'tm')), may hold values 0 or 1
- edge_feat: bfloat16 [8192, 128], P(('node', 'tm')), may hold values from -6 to 6
- msg_w1: bfloat16 [2176, 1024], replicated, may hold values from -0.125 to 0.125
- msg_b1: float32 [1024], replicated, may hold values from -4 to 4
- msg_w2: bfloat16 [1024, 1024], replicated, may hold values from -0.1875 to 0.1875
- msg_b2: float32 [1024], replicated, may hold values from -3 to 3
- gru_in: bfloat16 [1024, 3072], replicated, may hold values from -0.1875 to 0.1875
- gru_hid: bfloat16 [1024, 3072], replicated, may hold values from -0.1875 to 0.1875
- gru_bias: float32 [3072], replicated, may hold values from -3 to 3
Outputs:
- new_memory: bfloat16 [32768, 1024], P(('node', 'tm'))
The draws below stay inside these ranges and needn't reach their ends.
Inputs may be any that keep to these rules, and one draw needn't show every extreme that they name: `ends_owner`: within the events of one device (aligned blocks of 256 rows) no device is named by more than 20 endpoints, and some device by exactly 20; an event's two endpoints have different owners.
All inputs are finite; a program needn't handle non-finite values. No bound on the sum of `event_mask` on one device may be relied on, other than what follows from the above.
Results may differ from the reference program's by a relative error of at most 0.0026.
Values may be sent and summed in bfloat16 or wider, within the bound.
A program may use at most 128 MiB of HBM per device.

```python
import math
import jax
import jax.numpy as jnp
import numpy as np
from jax import lax

DM = 1024
HID = 1024
FE = 128
NODE_DEV = 1024
E_DEV = 256
CAP = 20
EVENTS = 8192
NODES = 32768
DEVICES = 32


def set_ends(drawn, key, smallest, largest):
    index_at = [jax.random.randint(jax.random.fold_in(key, axis), (), 0, length) for axis, length in enumerate(drawn.shape)]
    main_axis = drawn.shape.index(max(drawn.shape))
    neighbour = index_at[:main_axis] + [(index_at[main_axis] + 1) % drawn.shape[main_axis]] + index_at[main_axis + 1:]
    return drawn.at[tuple(index_at)].set(smallest).at[tuple(neighbour)].set(largest)


def block_levels(stream_key, dims, cuts, smallest, largest):
    def one(dim, parts):
        steps = jax.random.uniform(jax.random.fold_in(jax.random.fold_in(stream_key, 6), dim), (parts,), jnp.float32, smallest / len(cuts), largest / len(cuts))
        return jnp.repeat(jnp.exp(steps), dims[dim] // parts).reshape((-1,) + (1,) * (len(dims) - dim - 1))

    loudness = one(*cuts[0])
    for cut in cuts[1:]:
        loudness = loudness * one(*cut)
    return loudness


def deal_out(rng, own, number, rows, amount, top, bound, skew):
    sequence = jax.random.permutation(rng, amount)
    heavy_load, ordinary = portions_of(amount, rows * top, bound, skew, True), portions_of(amount, rows * top, bound, skew, False)
    places = jnp.arange(amount)

    def named(sizes, rotation):
        used = int((sizes > 0).sum())
        fixed = max(1, used // 4)
        moved = fixed + (places - fixed + rotation * (used - fixed)) % max(1, amount - fixed)
        return jnp.zeros((amount,), jnp.int32).at[sequence[jnp.where(places < fixed, places, moved)]].set(jnp.asarray(sizes, jnp.int32))

    sizes = jnp.where(number % 4 == 0, named(heavy_load, number // 4), named(ordinary, number - number // 4 - 1))
    mixed = jax.random.permutation(jax.random.fold_in(own, 3), amount)
    source_of, sink = mixed[0:amount // 2 * 2:2], mixed[1:amount // 2 * 2:2]
    slack = jnp.minimum(sizes[source_of] - 1, bound - sizes[sink]) // 2
    slack = jnp.where((source_of == sequence[0]) | (sink == sequence[0]) | (sizes[sink] == 0), 0, jnp.maximum(slack, 0))
    moved = jax.random.randint(jax.random.fold_in(own, 4), (amount // 2,), 0, 1 << 20) % (slack + 1)
    sizes = sizes.at[source_of].add(-moved).at[sink].add(moved)
    items = jnp.searchsorted(jnp.cumsum(sizes), jnp.arange(rows * top), side="right").astype(jnp.int32)
    listing = items.reshape(top, rows).T
    listing = listing[jax.random.permutation(jax.random.fold_in(own, 1), rows)]
    rotation = jax.random.randint(jax.random.fold_in(own, 2), (rows, 1), 0, top)
    return jnp.take_along_axis(listing, (jnp.arange(top)[None, :] + rotation) % top, axis=1)


def portions_of(amount, total, most, lean, full):
    loads = [(1 << 20) // math.isqrt(rank ** lean) + 1 for rank in range(1, amount + 1)]
    largest = most if full else min(most, max(-(-total // amount), total * loads[0] // sum(loads)))
    least = 1 if total - largest >= amount - 1 else 0
    holding, rest = [largest] + [least] * (amount - 1), total - largest - least * (amount - 1)
    while rest > 0:
        movable = [i for i in range(1, amount) if holding[i] < largest] or [i for i in range(1, amount) if holding[i] < most]
        mass, left = sum([loads[i] for i in movable]), rest
        for i in movable:
            extra = min(most - holding[i], max(1, left * loads[i] // mass), rest)
            holding[i] = holding[i] + extra
            rest = rest - extra
    return np.array(holding)


def gaussian(key, extent, spread, most, cuts=(), kind=jnp.bfloat16):
    gain = block_levels(key, extent, cuts, -0.22, 0.18) if cuts else 1.0
    result = jax.random.normal(key, extent, jnp.float32) * spread * gain
    return jnp.minimum(jnp.maximum(result, -most), most).astype(kind)


def setup_inputs(seed: int = 0) -> dict:
    splits = jax.random.split(jax.random.key(seed), 13)
    memory = gaussian(splits[0], (NODES, DM), 1.0, 6.0, ((0, 32),))
    ends_owner_keys = jax.random.split(jax.random.fold_in(splits[1], 1), EVENTS // E_DEV)
    ends_owner_turns = jax.random.permutation(jax.random.fold_in(splits[1], 3), EVENTS // E_DEV)
    ends_owner = jax.vmap(lambda own, number: deal_out(jax.random.fold_in(splits[1], 2), own, number, E_DEV, DEVICES, 2, CAP, 1))(ends_owner_keys, ends_owner_turns).reshape((EVENTS, 2))
    ends_row = set_ends(jax.random.randint(splits[2], (EVENTS, 2), 0, NODE_DEV), jax.random.fold_in(splits[2], 1), 0, NODE_DEV - 1).astype(jnp.int32)
    event_mask = set_ends((jax.random.randint(splits[3], (EVENTS,), 0, 4) < 3).astype(jnp.int32), jax.random.fold_in(splits[3], 1), 0, 1)
    edge_feat = gaussian(splits[4], (EVENTS, FE), 1.0, 6.0, ((0, 32),))
    msg_w1 = gaussian(splits[5], (2 * DM + FE, HID), (2 * DM + FE) ** -0.5, 0.125)
    msg_b1 = gaussian(splits[6], (HID,), 1.0, 4.0, (), jnp.float32)
    msg_w2 = gaussian(splits[7], (HID, DM), HID ** -0.5, 0.1875)
    msg_b2 = gaussian(splits[8], (DM,), 0.5, 3.0, (), jnp.float32)
    gru_in = gaussian(splits[9], (DM, 3 * DM), DM ** -0.5, 0.1875)
    gru_hid = gaussian(splits[10], (DM, 3 * DM), DM ** -0.5, 0.1875)
    gru_bias = gaussian(splits[11], (3 * DM,), 0.5, 3.0, (), jnp.float32)
    return dict(memory=memory, ends_owner=ends_owner, ends_row=ends_row, event_mask=event_mask, edge_feat=edge_feat, msg_w1=msg_w1, msg_b1=msg_b1, msg_w2=msg_w2, msg_b2=msg_b2, gru_in=gru_in, gru_hid=gru_hid, gru_bias=gru_bias)


def memory_update(aggregate, memory, gru_in, gru_hid, gru_bias, touched):
    feature_width = memory.shape[1]
    gates_in = jnp.dot(aggregate, gru_in, preferred_element_type=jnp.float32) + gru_bias
    gates_hid = jnp.dot(memory, gru_hid, preferred_element_type=jnp.float32)
    reset = jax.nn.sigmoid(gates_in[:, :feature_width] + gates_hid[:, :feature_width])
    update = jax.nn.sigmoid(gates_in[:, feature_width:2 * feature_width] + gates_hid[:, feature_width:2 * feature_width])
    candidate = jnp.tanh(gates_in[:, 2 * feature_width:] + reset * gates_hid[:, 2 * feature_width:])
    previous = memory.astype(jnp.float32)
    renewed = (1.0 - update) * candidate + update * previous
    return jnp.where(touched[:, None], renewed, previous).astype(jnp.bfloat16)


def reference(memory, ends_owner, ends_row, event_mask, edge_feat, msg_w1, msg_b1, msg_w2, msg_b2, gru_in, gru_hid, gru_bias):
    node_total = memory.shape[0]
    ids = (ends_owner * NODE_DEV + ends_row).astype(jnp.int32)
    block_ids = ids.reshape(-1, E_DEV, 2)
    block_mask = event_mask.reshape(-1, E_DEV)
    block_feat = edge_feat.reshape(-1, E_DEV, FE)

    def one_block(carry, item):
        summed, tally = carry
        bid, bmask, bfeat = item
        pairs = jnp.take(memory, bid.reshape(-1), axis=0).reshape(E_DEV, 2 * DM)
        inputs = jnp.concatenate([pairs, bfeat], axis=1)
        hidden = jax.nn.relu(jnp.dot(inputs, msg_w1, preferred_element_type=jnp.float32) + msg_b1).astype(jnp.bfloat16)
        weight_mask = bmask.astype(jnp.float32)
        message = ((jnp.dot(hidden, msg_w2, preferred_element_type=jnp.float32) + msg_b2) * weight_mask[:, None]).astype(jnp.bfloat16)
        summed = summed.at[bid[:, 1]].add(message.astype(jnp.float32))
        tally = tally.at[bid[:, 1]].add(weight_mask)
        return (summed, tally), None

    start = (jnp.zeros((node_total, DM), jnp.float32), jnp.zeros((node_total,), jnp.float32))
    (summed, tally), unused = lax.scan(one_block, start, (block_ids, block_mask, block_feat))
    aggregate = (summed / jnp.maximum(tally, 1.0)[:, None]).astype(jnp.bfloat16)

    def one_owner(item):
        agg_rows, mem_rows, tally_rows = item
        return memory_update(agg_rows, mem_rows, gru_in, gru_hid, gru_bias, tally_rows > 0.5)

    renewed = lax.map(one_owner, (aggregate.reshape(-1, NODE_DEV, DM), memory.reshape(-1, NODE_DEV, DM), tally.reshape(-1, NODE_DEV)))
    return renewed.reshape(node_total, DM)
```

```python
import functools

import jax
import jax.numpy as jnp
from jax import lax
from jax.experimental import pallas as pl
from jax.experimental.pallas import tpu as pltpu
from jax.sharding import PartitionSpec as P

BF = jnp.bfloat16
F32 = jnp.float32
I32 = jnp.int32
QUARTERS = 4
FIELDS = 8
TILE = 256


def div(x, n):
    if n & (n - 1) == 0:
        return lax.shift_right_logical(x, jnp.full_like(x, n.bit_length() - 1))
    return lax.div(x, jnp.full_like(x, n))


def rem(x, n):
    if n & (n - 1) == 0:
        return lax.bitwise_and(x, jnp.full_like(x, n - 1))
    return lax.rem(x, jnp.full_like(x, n))


def iota(rows, columns, axis):
    return lax.broadcasted_iota(I32, (rows, columns), axis)


def ones_where(condition):
    return jnp.where(condition, 1.0, 0.0).astype(BF)


def dot(a, b):
    return jnp.dot(a, b, preferred_element_type=F32)


def to_column(row):
    n = row.shape[1]
    return jnp.sum(jnp.where(iota(n, n, 0) == iota(n, n, 1), row, 0.0), axis=1, keepdims=True)


def to_row(column):
    n = column.shape[0]
    return jnp.sum(jnp.where(iota(n, n, 0) == iota(n, n, 1), column, 0.0), axis=0, keepdims=True)


def kernel(
    cfg,
    owner_ref, row_ref, mask_ref, feat_ref, b1_ref, b2_ref, gb_ref,
    mem_hbm, w1_hbm, w2_hbm, wi_hbm, wh_hbm,
    out_ref,
    mem, w1, w2, wi, wh, gh, table_out, table_in, fetched, hidden, tally, agg,
    main_row, main_flag, tail_row, tail_flag, tail_acc,
    ans_main, ret_main, msg_main, inc_main, ans_tail, ret_tail, msg_tail, inc_tail,
    load_sem, send_sem, recv_sem, own_sem,
):
    D, tm, m, R = cfg
    N, DM = mem.shape
    E = owner_ref.shape[1]
    HID = hidden.shape[1]
    QW = DM // QUARTERS
    tr = QUARTERS * R
    me = lax.axis_index("node") * tm + lax.axis_index("tm")

    loads = []
    for i, (src, dst) in enumerate(
        ((mem_hbm, mem), (wh_hbm, wh), (w1_hbm, w1), (w2_hbm, w2), (wi_hbm, wi))
    ):
        c = pltpu.make_async_copy(src, dst, load_sem.at[i])
        c.start()
        loads.append(c)

    barrier = pltpu.get_barrier_semaphore()

    @pl.loop(1, D)
    def _(i):
        peer = lax.rem(me + i, D)
        pl.semaphore_signal(
            barrier, inc=1, device_id=(peer // tm, lax.rem(peer, tm)),
            device_id_type=pl.DeviceIdType.MESH,
        )

    def start_exchange(k, pieces):
        for n, (src, dst, rows) in enumerate(pieces):
            pltpu.make_async_copy(
                src.at[pl.ds(pl.multiple_of(me * rows, rows), rows)],
                dst.at[pl.ds(pl.multiple_of(me * rows, rows), rows)],
                own_sem.at[k + n],
            ).start()

        @pl.loop(1, D)
        def _(i):
            peer = lax.rem(me + i, D)
            for n, (src, dst, rows) in enumerate(pieces):
                pltpu.make_async_remote_copy(
                    src_ref=src.at[pl.ds(pl.multiple_of(peer * rows, rows), rows)],
                    dst_ref=dst.at[pl.ds(pl.multiple_of(me * rows, rows), rows)],
                    send_sem=send_sem.at[k + n],
                    recv_sem=recv_sem.at[k + n],
                    device_id=(peer // tm, lax.rem(peer, tm)),
                    device_id_type=pl.DeviceIdType.MESH,
                ).start()

    def wait_received(k, pieces):
        for n, (src, dst, rows) in enumerate(pieces):
            part = dst.at[pl.ds(0, (D - 1) * rows)]
            pltpu.make_async_copy(part, part, recv_sem.at[k + n]).wait()
            own = dst.at[pl.ds(0, rows)]
            pltpu.make_async_copy(own, own, own_sem.at[k + n]).wait()

    def wait_sent(k, pieces):
        for n, (src, dst, rows) in enumerate(pieces):
            part = src.at[pl.ds(0, (D - 1) * rows)]
            pltpu.make_async_copy(part, part, send_sem.at[k + n]).wait()

    tables = [(table_out, table_in, FIELDS)]
    answers = [(ans_tail, ret_tail, tr)]
    messages = [(msg_tail, inc_tail, tr)]
    if m:
        answers.append((ans_main, ret_main, m))
        messages.append((msg_main, inc_main, m))

    owner = jnp.concatenate([owner_ref[0:1, :], owner_ref[1:2, :]], axis=1)
    wanted = jnp.concatenate([row_ref[0:1, :], row_ref[1:2, :]], axis=1)
    flag = jnp.concatenate([jnp.zeros((1, E), I32), mask_ref[...]], axis=1)
    onehot = jnp.where(iota(D, 2 * E, 0) == owner, 1.0, 0.0)
    earlier = ones_where(iota(2 * E, 2 * E, 0) < iota(2 * E, 2 * E, 1))
    position = jnp.sum(onehot * dot(onehot.astype(BF), earlier), axis=0, keepdims=True).astype(I32)
    field = rem(iota(D * FIELDS, 2 * E, 0), FIELDS)
    value = jnp.where(
        field == 0, div(wanted, 32) + 1,
        jnp.where(field == 1, rem(wanted, 32), jnp.where(field == 2, flag, 0)),
    )
    value = jnp.where(div(iota(D * FIELDS, 2 * E, 0), FIELDS) == owner, value, 0)
    place = ones_where(iota(128, 2 * E, 0) == position)
    table_out[...] = lax.dot_general(
        value.astype(F32).astype(BF), place, (((1,), (1,)), ((), ())), preferred_element_type=F32
    )
    pl.semaphore_wait(barrier, D - 1)
    start_exchange(0, tables)

    far = -4 * D * (m + tr)
    at_main = jnp.where(position < m, owner * m + position, far)
    at_tail = jnp.where(position >= m, owner * tr + position - m, far)
    main_column = to_column(at_main.astype(F32)).astype(I32)
    tail_column = to_column(at_tail.astype(F32)).astype(I32)
    sent_main = jnp.where(flag[:, E:] > 0, at_main[:, E:], far)
    sent_tail = jnp.where(flag[:, E:] > 0, at_tail[:, E:], far)

    loads[0].wait()
    wait_received(0, tables)

    table = table_in[...].astype(BF)

    def slots(base, size, block, first, period):
        s = base + iota(size, D * FIELDS, 0)
        field_row = iota(size, D * FIELDS, 1)
        start = div(s, block) * FIELDS
        pick = jnp.where(field_row == start, 32.0, jnp.where(field_row == start + 1, 1.0, 0.0))
        lane = iota(size, 128, 1) == first + rem(base + iota(size, 128, 0), period)
        ids = jnp.sum(jnp.where(lane, dot(pick.astype(BF), table), 0.0), axis=1, keepdims=True)
        marks = jnp.sum(
            jnp.where(lane, dot(ones_where(field_row == start + 2), table), 0.0),
            axis=1, keepdims=True,
        )
        return ids - 32.0, marks

    chunk = min(512, D * tr)

    @pl.loop(0, D * tr // chunk)
    def _(step):
        base = pl.multiple_of(step * chunk, chunk)
        ids, marks = slots(base, chunk, tr, m, R)
        quarter = rem(div(base + iota(chunk, 1, 0), R), QUARTERS)
        tail_row[:, pl.ds(base, chunk)] = to_row(ids).astype(I32)
        tail_flag[:, pl.ds(base, chunk)] = to_row(jnp.where(quarter == 0, marks, 0.0))
        total = jnp.zeros((chunk, QW), F32)
        nodes = iota(chunk, N, 1)
        for q in range(QUARTERS):
            hit = ones_where(nodes == jnp.where(quarter == q, ids.astype(I32), -1))
            total = total + dot(hit, mem[:, q * QW : (q + 1) * QW])
        ans_tail[pl.ds(base, chunk), :] = total.astype(BF)

    if m:
        main_chunk = min(512, D * m)

        @pl.loop(0, D * m // main_chunk)
        def _(step):
            base = pl.multiple_of(step * main_chunk, main_chunk)
            ids, marks = slots(base, main_chunk, m, 0, m)
            main_row[:, pl.ds(base, main_chunk)] = to_row(ids).astype(I32)
            main_flag[:, pl.ds(base, main_chunk)] = to_row(marks)
            hit = ones_where(iota(main_chunk, N, 1) == ids.astype(I32))

            @pl.loop(0, QUARTERS)
            def _(q):
                cols = pl.ds(pl.multiple_of(q * QW, QW), QW)
                ans_main[pl.ds(base, main_chunk), cols] = dot(hit, mem[:, cols]).astype(BF)

    start_exchange(1, answers)

    loads[1].wait()

    @pl.loop(0, 3 * DM // TILE)
    def _(t):
        cols = pl.ds(pl.multiple_of(t * TILE, TILE), TILE)
        gh[:, cols] = dot(mem[...], wh[:, cols])

    @pl.loop(0, N // TILE)
    def _(t):
        base = pl.multiple_of(t * TILE, TILE)
        nodes = base + iota(TILE, D * tr, 0)
        count = jnp.sum(jnp.where(tail_row[...] == nodes, tail_flag[...], 0.0), axis=1, keepdims=True)
        if m:
            nodes = base + iota(TILE, D * m, 0)
            count = count + jnp.sum(
                jnp.where(main_row[...] == nodes, main_flag[...], 0.0), axis=1, keepdims=True
            )
        tally[pl.ds(base, TILE), :] = count

    loads[2].wait()
    loads[3].wait()
    wait_received(1, answers)

    if m:
        from_main = ones_where(iota(2 * E, D * m, 1) == main_column)

    @pl.loop(0, QUARTERS)
    def _(q):
        cols = pl.ds(pl.multiple_of(q * QW, QW), QW)
        got = dot(ones_where(iota(2 * E, D * tr, 1) == tail_column + q * R), ret_tail[...])
        if m:
            got = got + dot(from_main, ret_main[:, cols])
        fetched[:, cols] = got.astype(BF)

    @pl.loop(0, HID // TILE)
    def _(t):
        cols = pl.ds(pl.multiple_of(t * TILE, TILE), TILE)
        h = dot(fetched[0:E, :], w1[0:DM, cols]) + dot(fetched[E : 2 * E, :], w1[DM : 2 * DM, cols])
        h = h + dot(feat_ref[...], w1[2 * DM :, cols]) + b1_ref[:, cols]
        hidden[:, cols] = jnp.maximum(h, 0.0).astype(BF)

    tail_acc[...] = jnp.zeros_like(tail_acc)
    if m:
        to_main = ones_where(iota(D * m, E, 0) == sent_main)

    @pl.loop(0, QUARTERS)
    def _(q):
        cols = pl.ds(pl.multiple_of(q * QW, QW), QW)
        message = (dot(hidden[...], w2[:, cols]) + b2_ref[:, cols]).astype(BF)
        if m:
            msg_main[:, cols] = dot(to_main, message).astype(BF)
        tail_acc[...] += dot(ones_where(iota(D * tr, E, 0) == sent_tail + q * R), message)

    msg_tail[...] = tail_acc[...].astype(BF)
    k = 1 + len(answers)
    start_exchange(k, messages)
    wait_sent(0, tables)
    wait_sent(1, answers)
    loads[4].wait()
    wait_received(k, messages)

    @pl.loop(0, N // TILE)
    def _(t):
        base = pl.multiple_of(t * TILE, TILE)
        rows = pl.ds(base, TILE)
        count = tally[rows, :]
        nodes = base + iota(TILE, D * tr, 0)
        quarter = rem(div(iota(1, D * tr, 1), R), QUARTERS)
        if m:
            hit_main = ones_where(main_row[...] == base + iota(TILE, D * m, 0))

        @pl.loop(0, QUARTERS)
        def _(q):
            cols = pl.ds(pl.multiple_of(q * QW, QW), QW)
            hit = ones_where(jnp.where(quarter == q, tail_row[...], -1) == nodes)
            summed = dot(hit, inc_tail[...])
            if m:
                summed = summed + dot(hit_main, inc_main[:, cols])
            agg[:, cols] = (summed / jnp.maximum(count, 1.0)).astype(BF)

        @pl.loop(0, DM // TILE)
        def _(c):
            def part(g):
                cols = pl.ds(pl.multiple_of(g * DM + c * TILE, TILE), TILE)
                return dot(agg[...], wi[:, cols]) + gb_ref[:, cols], gh[rows, cols]

            cols = pl.ds(pl.multiple_of(c * TILE, TILE), TILE)
            gi_r, gh_r = part(0)
            gi_z, gh_z = part(1)
            gi_c, gh_c = part(2)
            reset = 0.5 * jnp.tanh(0.5 * (gi_r + gh_r)) + 0.5
            update = 0.5 * jnp.tanh(0.5 * (gi_z + gh_z)) + 0.5
            candidate = jnp.tanh(gi_c + reset * gh_c)
            previous = mem[rows, cols].astype(F32)
            renewed = (1.0 - update) * candidate + update * previous
            out_ref[rows, cols] = jnp.where(count > 0.5, renewed, previous).astype(BF)

    wait_sent(k, messages)


def on_device(
    mesh_sizes,
    memory,
    ends_owner,
    ends_row,
    event_mask,
    edge_feat,
    msg_w1,
    msg_b1,
    msg_w2,
    msg_b2,
    gru_in,
    gru_hid,
    gru_bias,
):
    D, tm = mesh_sizes
    E = ends_owner.shape[0]
    N, DM = memory.shape
    HID = msg_w2.shape[0]
    cap = 5 * E // (2 * D)
    m = cap // 16 * 16
    R = max(4, -(-(cap - m) // 4) * 4)
    tr = QUARTERS * R
    QW = DM // QUARTERS
    mains = max(m, 1) * D if m else 16
    vmem = pl.BlockSpec(memory_space=pltpu.VMEM)
    anywhere = pl.BlockSpec(memory_space=pl.ANY)
    return pl.pallas_call(
        functools.partial(kernel, (D, tm, m, R)),
        out_shape=jax.ShapeDtypeStruct((N, DM), BF),
        in_specs=[vmem] * 7 + [anywhere] * 5,
        out_specs=vmem,
        scratch_shapes=[
            pltpu.VMEM(memory.shape, BF),
            pltpu.VMEM(msg_w1.shape, BF),
            pltpu.VMEM(msg_w2.shape, BF),
            pltpu.VMEM(gru_in.shape, BF),
            pltpu.VMEM(gru_hid.shape, BF),
            pltpu.VMEM((N, 3 * DM), F32),
            pltpu.VMEM((D * FIELDS, 128), F32),
            pltpu.VMEM((D * FIELDS, 128), F32),
            pltpu.VMEM((2 * E, DM), BF),
            pltpu.VMEM((E, HID), BF),
            pltpu.VMEM((N, 1), F32),
            pltpu.VMEM((TILE, DM), BF),
            pltpu.VMEM((1, mains), I32),
            pltpu.VMEM((1, mains), F32),
            pltpu.VMEM((1, D * tr), I32),
            pltpu.VMEM((1, D * tr), F32),
            pltpu.VMEM((D * tr, QW), F32),
        ]
        + [pltpu.VMEM((mains, DM), BF)] * 4
        + [pltpu.VMEM((D * tr, QW), BF)] * 4
        + [
            pltpu.SemaphoreType.DMA((5,)),
            pltpu.SemaphoreType.DMA((5,)),
            pltpu.SemaphoreType.DMA((5,)),
            pltpu.SemaphoreType.DMA((5,)),
        ],
        compiler_params=pltpu.CompilerParams(
            collective_id=0, has_side_effects=True, vmem_limit_bytes=60 * 2**20
        ),
    )(
        ends_owner.T,
        ends_row.T,
        event_mask.reshape(1, E),
        edge_feat,
        msg_b1.reshape(1, -1),
        msg_b2.reshape(1, -1),
        gru_bias.reshape(1, -1),
        memory,
        msg_w1,
        msg_w2,
        gru_in,
        gru_hid,
    )


def solution(mesh):
    sizes = (mesh.shape["node"] * mesh.shape["tm"], mesh.shape["tm"])
    split = P(("node", "tm"))
    return jax.shard_map(
        functools.partial(on_device, sizes),
        mesh=mesh,
        in_specs=(split,) * 5 + (P(),) * 7,
        out_specs=split,
        check_vma=False,
    )
```

```python
import functools

import jax
import jax.numpy as jnp
from jax import lax
from jax.experimental import pallas as pl
from jax.experimental.pallas import tpu as pltpu
from jax.sharding import PartitionSpec as P

BF = jnp.bfloat16
F32 = jnp.float32
I32 = jnp.int32
QUARTERS = 4
FIELDS = 8
TILE = 256
HALVES = 2


def div(x, n):
    if n & (n - 1) == 0:
        return lax.shift_right_logical(x, jnp.full_like(x, n.bit_length() - 1))
    return lax.div(x, jnp.full_like(x, n))


def rem(x, n):
    if n & (n - 1) == 0:
        return lax.bitwise_and(x, jnp.full_like(x, n - 1))
    return lax.rem(x, jnp.full_like(x, n))


def iota(rows, columns, axis):
    return lax.broadcasted_iota(I32, (rows, columns), axis)


def ones_where(condition):
    return jnp.where(condition, 1.0, 0.0).astype(BF)


def dot(a, b):
    return jnp.dot(a, b, preferred_element_type=F32)


def to_column(row):
    n = row.shape[1]
    return jnp.sum(jnp.where(iota(n, n, 0) == iota(n, n, 1), row, 0.0), axis=1, keepdims=True)


def to_row(column):
    n = column.shape[0]
    return jnp.sum(jnp.where(iota(n, n, 0) == iota(n, n, 1), column, 0.0), axis=0, keepdims=True)


def kernel(
    cfg,
    owner_ref, row_ref, mask_ref, feat_ref, b1_ref, b2_ref,
    mem_hbm, w1_hbm, w2_hbm, wh_hbm,
    agg_out, gh_out, held_out, rank_out, total_out,
    mem, w1, w2, wh, gh, held, table_out, table_in, fetched, acc, hidden, tally,
    main_row, main_flag, tail_row, tail_flag, tail_acc, sums,
    ans_main, ret_main, msg_main, inc_main, ans_tail, ret_tail, msg_tail, inc_tail,
    load_sem, send_sem, recv_sem, own_sem, store_sem,
):
    D, tm, m, R = cfg
    N, DM = mem.shape
    E = owner_ref.shape[1]
    HID = hidden.shape[1]
    QW = DM // QUARTERS
    HW = DM // HALVES
    tr = QUARTERS * R
    ranks = agg_out.shape[0]
    me = lax.axis_index("node") * tm + lax.axis_index("tm")

    loads = []
    for i, (src, dst) in enumerate(
        ((mem_hbm, mem), (wh_hbm, wh), (w1_hbm, w1), (w2_hbm, w2))
    ):
        c = pltpu.make_async_copy(src, dst, load_sem.at[i])
        c.start()
        loads.append(c)

    barrier = pltpu.get_barrier_semaphore()

    @pl.loop(1, D)
    def _(i):
        peer = lax.rem(me + i, D)
        pl.semaphore_signal(
            barrier, inc=1, device_id=(peer // tm, lax.rem(peer, tm)),
            device_id_type=pl.DeviceIdType.MESH,
        )

    def start_exchange(k, pieces):
        for n, (src, dst, rows) in enumerate(pieces):
            pltpu.make_async_copy(
                src.at[pl.ds(pl.multiple_of(me * rows, rows), rows)],
                dst.at[pl.ds(pl.multiple_of(me * rows, rows), rows)],
                own_sem.at[k + n],
            ).start()

        @pl.loop(1, D)
        def _(i):
            peer = lax.rem(me + i, D)
            for n, (src, dst, rows) in enumerate(pieces):
                pltpu.make_async_remote_copy(
                    src_ref=src.at[pl.ds(pl.multiple_of(peer * rows, rows), rows)],
                    dst_ref=dst.at[pl.ds(pl.multiple_of(me * rows, rows), rows)],
                    send_sem=send_sem.at[k + n],
                    recv_sem=recv_sem.at[k + n],
                    device_id=(peer // tm, lax.rem(peer, tm)),
                    device_id_type=pl.DeviceIdType.MESH,
                ).start()

    def wait_received(k, pieces):
        for n, (src, dst, rows) in enumerate(pieces):
            part = dst.at[pl.ds(0, (D - 1) * rows)]
            pltpu.make_async_copy(part, part, recv_sem.at[k + n]).wait()
            own = dst.at[pl.ds(0, rows)]
            pltpu.make_async_copy(own, own, own_sem.at[k + n]).wait()

    def wait_sent(k, pieces):
        for n, (src, dst, rows) in enumerate(pieces):
            part = src.at[pl.ds(0, (D - 1) * rows)]
            pltpu.make_async_copy(part, part, send_sem.at[k + n]).wait()

    tables = [(table_out, table_in, FIELDS)]
    ans_t = [(ans_tail, ret_tail, tr)]
    msg_t = [(msg_tail, inc_tail, tr)]
    ans_m = [[(ans_main.at[h], ret_main.at[h], m)] if m else [] for h in range(HALVES)]
    msg_m = [[(msg_main.at[h], inc_main.at[h], m)] if m else [] for h in range(HALVES)]

    owner = jnp.concatenate([owner_ref[0:1, :], owner_ref[1:2, :]], axis=1)
    wanted = jnp.concatenate([row_ref[0:1, :], row_ref[1:2, :]], axis=1)
    flag = jnp.concatenate([jnp.zeros((1, E), I32), mask_ref[...]], axis=1)
    onehot = jnp.where(iota(D, 2 * E, 0) == owner, 1.0, 0.0)
    earlier = ones_where(iota(2 * E, 2 * E, 0) < iota(2 * E, 2 * E, 1))
    position = jnp.sum(onehot * dot(onehot.astype(BF), earlier), axis=0, keepdims=True).astype(I32)
    field = rem(iota(D * FIELDS, 2 * E, 0), FIELDS)
    value = jnp.where(
        field == 0, div(wanted, 32) + 1,
        jnp.where(field == 1, rem(wanted, 32), jnp.where(field == 2, flag, 0)),
    )
    value = jnp.where(div(iota(D * FIELDS, 2 * E, 0), FIELDS) == owner, value, 0)
    place = ones_where(iota(128, 2 * E, 0) == position)
    table_out[...] = lax.dot_general(
        value.astype(F32).astype(BF), place, (((1,), (1,)), ((), ())), preferred_element_type=F32
    )
    pl.semaphore_wait(barrier, D - 1)
    start_exchange(0, tables)

    far = -4 * D * (m + tr)
    at_main = jnp.where(position < m, owner * m + position, far)
    at_tail = jnp.where(position >= m, owner * tr + position - m, far)
    main_column = to_column(at_main.astype(F32)).astype(I32)
    tail_column = to_column(at_tail.astype(F32)).astype(I32)
    sent_main = jnp.where(flag[:, E:] > 0, at_main[:, E:], far)
    sent_tail = jnp.where(flag[:, E:] > 0, at_tail[:, E:], far)

    loads[0].wait()
    wait_received(0, tables)

    table = table_in[...].astype(BF)

    def slots(base, size, block, first, period):
        s = base + iota(size, D * FIELDS, 0)
        field_row = iota(size, D * FIELDS, 1)
        start = div(s, block) * FIELDS
        pick = jnp.where(field_row == start, 32.0, jnp.where(field_row == start + 1, 1.0, 0.0))
        lane = iota(size, 128, 1) == first + rem(base + iota(size, 128, 0), period)
        ids = jnp.sum(jnp.where(lane, dot(pick.astype(BF), table), 0.0), axis=1, keepdims=True)
        marks = jnp.sum(
            jnp.where(lane, dot(ones_where(field_row == start + 2), table), 0.0),
            axis=1, keepdims=True,
        )
        return ids - 32.0, marks

    chunk = min(512, D * tr)

    @pl.loop(0, D * tr // chunk)
    def _(step):
        base = pl.multiple_of(step * chunk, chunk)
        ids, marks = slots(base, chunk, tr, m, R)
        quarter = rem(div(base + iota(chunk, 1, 0), R), QUARTERS)
        tail_row[:, pl.ds(base, chunk)] = to_row(ids).astype(I32)
        tail_flag[:, pl.ds(base, chunk)] = to_row(jnp.where(quarter == 0, marks, 0.0))
        total = jnp.zeros((chunk, QW), F32)
        nodes = iota(chunk, N, 1)
        for q in range(QUARTERS):
            hit = ones_where(nodes == jnp.where(quarter == q, ids.astype(I32), -1))
            total = total + dot(hit, mem[:, q * QW : (q + 1) * QW])
        ans_tail[pl.ds(base, chunk), :] = total.astype(BF)

    start_exchange(1, ans_t)

    if m:
        main_chunk = min(512, D * m)
        main_steps = D * m // main_chunk
        for h in range(HALVES):

            @pl.loop(0, main_steps)
            def _(step):
                base = pl.multiple_of(step * main_chunk, main_chunk)
                ids, marks = slots(base, main_chunk, m, 0, m)
                if h == 0:
                    main_row[:, pl.ds(base, main_chunk)] = to_row(ids).astype(I32)
                    main_flag[:, pl.ds(base, main_chunk)] = to_row(marks)
                hit = ones_where(iota(main_chunk, N, 1) == ids.astype(I32))
                ans_main[h, pl.ds(base, main_chunk), :] = dot(
                    hit, mem[:, h * HW : (h + 1) * HW]
                ).astype(BF)

            start_exchange(2 + h, ans_m[h])

    @pl.loop(0, N // TILE)
    def _(t):
        base = pl.multiple_of(t * TILE, TILE)
        nodes = base + iota(TILE, D * tr, 0)
        count = jnp.sum(jnp.where(tail_row[...] == nodes, tail_flag[...], 0.0), axis=1, keepdims=True)
        if m:
            nodes = base + iota(TILE, D * m, 0)
            count = count + jnp.sum(
                jnp.where(main_row[...] == nodes, main_flag[...], 0.0), axis=1, keepdims=True
            )
        tally[pl.ds(base, TILE), :] = count

    tally_row = to_row(tally[...])
    touched_row = jnp.where(tally_row > 0.5, 1.0, 0.0)
    earlier = ones_where(iota(N, N, 0) < iota(N, N, 1))
    before = dot(jnp.broadcast_to(touched_row, (8, N)).astype(BF), earlier)[0:1, :]
    rank_row = jnp.where(touched_row > 0.5, before, -1.0)
    rank_column = to_column(rank_row)
    rank_out[...] = jnp.broadcast_to(rank_column, (N, 128)).astype(I32)
    total_out[...] = jnp.broadcast_to(
        jnp.sum(touched_row, axis=1, keepdims=True), (8, 128)
    ).astype(I32)

    def rank_slots(row_ref, count, size):
        @pl.loop(0, count // size)
        def _(step):
            cols = pl.ds(pl.multiple_of(step * size, size), size)
            same = iota(N, size, 0) == row_ref[:, cols]
            row_ref[:, cols] = jnp.sum(
                jnp.where(same, rank_column, 0.0), axis=0, keepdims=True
            ).astype(I32)

    rank_slots(tail_row, D * tr, chunk)
    if m:
        rank_slots(main_row, D * m, main_chunk)

    loads[1].wait()

    @pl.loop(0, ranks // TILE)
    def _(t):
        base = pl.multiple_of(t * TILE, TILE)
        rows = pl.ds(base, TILE)
        pick = rank_row.astype(I32) == base + iota(TILE, N, 0)
        tally[rows, :] = jnp.sum(jnp.where(pick, tally_row, 0.0), axis=1, keepdims=True)
        pick = ones_where(pick)

        @pl.loop(0, DM // TILE)
        def _(c):
            cols = pl.ds(pl.multiple_of(c * TILE, TILE), TILE)
            held[rows, cols] = dot(pick, mem[:, cols]).astype(BF)

    @pl.loop(0, 3 * DM // TILE)
    def _(t):
        cols = pl.ds(pl.multiple_of(t * TILE, TILE), TILE)
        gh[:, cols] = dot(held[...], wh[:, cols])

    stores = [
        pltpu.make_async_copy(gh, gh_out, store_sem.at[0]),
        pltpu.make_async_copy(held, held_out, store_sem.at[1]),
    ]
    for c in stores:
        c.start()

    loads[2].wait()
    loads[3].wait()
    feat_width = feat_ref.shape[1]

    @pl.loop(0, HID // TILE)
    def _(t):
        cols = pl.ds(pl.multiple_of(t * TILE, TILE), TILE)
        acc[:, cols] = dot(feat_ref[...], w1[2 * DM : 2 * DM + feat_width, cols]) + b1_ref[:, cols]

    wait_received(1, ans_t)
    if m:
        from_main = ones_where(iota(2 * E, D * m, 1) == main_column)

    for h in range(HALVES):
        wait_received(2 + h, ans_m[h])
        got = []
        for q in range(h * QUARTERS // HALVES, (h + 1) * QUARTERS // HALVES):
            got.append(dot(ones_where(iota(2 * E, D * tr, 1) == tail_column + q * R), ret_tail[...]))
        got = jnp.concatenate(got, axis=1)
        if m:
            got = got + dot(from_main, ret_main[h])
        fetched[...] = got.astype(BF)

        @pl.loop(0, HID // TILE)
        def _(t):
            cols = pl.ds(pl.multiple_of(t * TILE, TILE), TILE)
            total = acc[:, cols] + dot(fetched[0:E, :], w1[h * HW : (h + 1) * HW, cols])
            total = total + dot(fetched[E : 2 * E, :], w1[DM + h * HW : DM + (h + 1) * HW, cols])
            if h == HALVES - 1:
                hidden[:, cols] = jnp.maximum(total, 0.0).astype(BF)
            else:
                acc[:, cols] = total

    tail_acc[...] = jnp.zeros_like(tail_acc)
    if m:
        to_main = ones_where(iota(D * m, E, 0) == sent_main)
    k = 2 + HALVES
    for h in range(HALVES):
        cols = slice(h * HW, (h + 1) * HW)
        message = (dot(hidden[...], w2[:, cols]) + b2_ref[:, cols]).astype(BF)
        if m:
            msg_main[h] = dot(to_main, message).astype(BF)
            start_exchange(k + 1 + h, msg_m[h])
        for j in range(QUARTERS // HALVES):
            q = h * QUARTERS // HALVES + j
            tail_acc[...] += dot(
                ones_where(iota(D * tr, E, 0) == sent_tail + q * R),
                message[:, j * QW : (j + 1) * QW],
            )

    msg_tail[...] = tail_acc[...].astype(BF)
    start_exchange(k, msg_t)
    wait_sent(0, tables)
    wait_sent(1, ans_t)
    for h in range(HALVES):
        wait_sent(2 + h, ans_m[h])
    for c in stores:
        c.wait()

    quarter = rem(div(iota(1, D * tr, 1), R), QUARTERS)
    for h in range(HALVES):
        wait_received(k + 1 + h, msg_m[h])
        if h == HALVES - 1:
            wait_received(k, msg_t)
        if m:

            @pl.loop(0, ranks // TILE)
            def _(t):
                base = pl.multiple_of(t * TILE, TILE)
                rows = pl.ds(base, TILE)
                hit = ones_where(main_row[...] == base + iota(TILE, D * m, 0))
                sums[rows, h * HW : (h + 1) * HW] = dot(hit, inc_main[h])

    @pl.loop(0, ranks // TILE)
    def _(t):
        base = pl.multiple_of(t * TILE, TILE)
        rows = pl.ds(base, TILE)
        count = jnp.maximum(tally[rows, :], 1.0)
        for q in range(QUARTERS):
            cols = slice(q * QW, (q + 1) * QW)
            wanted_rank = base + iota(TILE, D * tr, 0)
            hit = ones_where(jnp.where(quarter == q, tail_row[...], -1) == wanted_rank)
            summed = dot(hit, inc_tail[...])
            if m:
                summed = summed + sums[rows, cols]
            agg_out[rows, cols] = (summed / count).astype(BF)

    wait_sent(k, msg_t)
    for h in range(HALVES):
        wait_sent(k + 1 + h, msg_m[h])


def gru_kernel(
    total_ref, rank_ref, gb_ref, mem_ref, agg_hbm, gh_hbm, held_hbm, wi_hbm,
    out_ref,
    agg, gh, held, wi, fresh, load_sem, weight_sem,
):
    N, DM = mem_ref.shape
    steps = DM // TILE
    tiles = lax.div(total_ref[0, 0] + (TILE - 1), TILE)

    def tile_copies(t):
        rows = pl.ds(pl.multiple_of(t * TILE, TILE), TILE)
        return [
            pltpu.make_async_copy(agg_hbm.at[rows], agg, load_sem.at[0]),
            pltpu.make_async_copy(gh_hbm.at[rows], gh, load_sem.at[1]),
            pltpu.make_async_copy(held_hbm.at[rows], held, load_sem.at[2]),
        ]

    def weight_copies(c):
        copies = []
        for g in range(3):
            cols = pl.ds(g * DM + c * TILE, TILE)
            copies.append(
                pltpu.make_async_copy(wi_hbm.at[:, cols], wi.at[:, cols], weight_sem.at[c, g])
            )
        return copies

    for c in tile_copies(0):
        c.start()
    for c in range(steps):
        for copy in weight_copies(c):
            copy.start()
    out_ref[...] = mem_ref[...]
    for c in tile_copies(0):
        c.wait()

    def one_step(c):
        def part(g):
            cols = slice(g * DM + c * TILE, g * DM + (c + 1) * TILE)
            return dot(agg[...], wi[:, cols]) + gb_ref[:, cols], gh[:, cols]

        cols = slice(c * TILE, (c + 1) * TILE)
        gi_r, gh_r = part(0)
        gi_z, gh_z = part(1)
        gi_c, gh_c = part(2)
        reset = 0.5 * jnp.tanh(0.5 * (gi_r + gh_r)) + 0.5
        update = 0.5 * jnp.tanh(0.5 * (gi_z + gh_z)) + 0.5
        candidate = jnp.tanh(gi_c + reset * gh_c)
        previous = held[:, cols].astype(F32)
        fresh[:, cols] = ((1.0 - update) * candidate + update * previous).astype(BF)

    def spread(base):
        column = rank_ref[:, 0:1] - base
        place = ones_where(column == iota(N, TILE, 1))
        mine = (column >= 0) & (column < TILE)

        @pl.loop(0, steps)
        def _(c):
            cols = pl.ds(pl.multiple_of(c * TILE, TILE), TILE)
            moved = dot(place, fresh[:, cols])
            out_ref[:, cols] = jnp.where(mine, moved, out_ref[:, cols].astype(F32)).astype(BF)

    for c in range(steps):
        for copy in weight_copies(c):
            copy.wait()
        one_step(c)
    spread(0)

    @pl.loop(1, tiles)
    def _(t):
        for c in tile_copies(t):
            c.start()
        for c in tile_copies(t):
            c.wait()
        for c in range(steps):
            one_step(c)
        spread(t * TILE)


def on_device(
    mesh_sizes,
    memory,
    ends_owner,
    ends_row,
    event_mask,
    edge_feat,
    msg_w1,
    msg_b1,
    msg_w2,
    msg_b2,
    gru_in,
    gru_hid,
    gru_bias,
):
    D, tm = mesh_sizes
    E = ends_owner.shape[0]
    N, DM = memory.shape
    HID = msg_w2.shape[0]
    cap = 5 * E // (2 * D)
    m = cap // 16 * 16
    R = max(4, -(-(cap - m) // 4) * 4)
    tr = QUARTERS * R
    QW = DM // QUARTERS
    mains = D * m if m else 16
    ranks = -(-min(N, D * cap) // TILE) * TILE
    vmem = pl.BlockSpec(memory_space=pltpu.VMEM)
    smem = pl.BlockSpec(memory_space=pltpu.SMEM)
    anywhere = pl.BlockSpec(memory_space=pl.ANY)
    phases = 3 + 2 * HALVES
    agg, gh, held, rank, total = pl.pallas_call(
        functools.partial(kernel, (D, tm, m, R)),
        out_shape=[
            jax.ShapeDtypeStruct((ranks, DM), BF),
            jax.ShapeDtypeStruct((ranks, 3 * DM), F32),
            jax.ShapeDtypeStruct((ranks, DM), BF),
            jax.ShapeDtypeStruct((N, 128), I32),
            jax.ShapeDtypeStruct((8, 128), I32),
        ],
        in_specs=[vmem] * 6 + [anywhere] * 4,
        out_specs=[vmem, anywhere, anywhere, vmem, vmem],
        scratch_shapes=[
            pltpu.VMEM(memory.shape, BF),
            pltpu.VMEM(msg_w1.shape, BF),
            pltpu.VMEM(msg_w2.shape, BF),
            pltpu.VMEM(gru_hid.shape, BF),
            pltpu.VMEM((ranks, 3 * DM), F32),
            pltpu.VMEM((ranks, DM), BF),
            pltpu.VMEM((D * FIELDS, 128), F32),
            pltpu.VMEM((D * FIELDS, 128), F32),
            pltpu.VMEM((2 * E, DM // HALVES), BF),
            pltpu.VMEM((E, HID), F32),
            pltpu.VMEM((E, HID), BF),
            pltpu.VMEM((N, 1), F32),
            pltpu.VMEM((1, mains), I32),
            pltpu.VMEM((1, mains), F32),
            pltpu.VMEM((1, D * tr), I32),
            pltpu.VMEM((1, D * tr), F32),
            pltpu.VMEM((D * tr, QW), F32),
            pltpu.VMEM((ranks, DM), F32),
        ]
        + [pltpu.VMEM((HALVES, mains, DM // HALVES), BF)] * 4
        + [pltpu.VMEM((D * tr, QW), BF)] * 4
        + [
            pltpu.SemaphoreType.DMA((4,)),
            pltpu.SemaphoreType.DMA((phases,)),
            pltpu.SemaphoreType.DMA((phases,)),
            pltpu.SemaphoreType.DMA((phases,)),
            pltpu.SemaphoreType.DMA((2,)),
        ],
        compiler_params=pltpu.CompilerParams(
            collective_id=0, has_side_effects=True, vmem_limit_bytes=48 * 2**20
        ),
    )(
        ends_owner.T,
        ends_row.T,
        event_mask.reshape(1, E),
        edge_feat,
        msg_b1.reshape(1, -1),
        msg_b2.reshape(1, -1),
        memory,
        msg_w1,
        msg_w2,
        gru_hid,
    )
    return pl.pallas_call(
        gru_kernel,
        out_shape=jax.ShapeDtypeStruct((N, DM), BF),
        in_specs=[smem, vmem, vmem, vmem] + [anywhere] * 4,
        out_specs=vmem,
        scratch_shapes=[
            pltpu.VMEM((TILE, DM), BF),
            pltpu.VMEM((TILE, 3 * DM), F32),
            pltpu.VMEM((TILE, DM), BF),
            pltpu.VMEM(gru_in.shape, BF),
            pltpu.VMEM((TILE, DM), BF),
            pltpu.SemaphoreType.DMA((3,)),
            pltpu.SemaphoreType.DMA((DM // TILE, 3)),
        ],
        compiler_params=pltpu.CompilerParams(vmem_limit_bytes=40 * 2**20),
    )(total, rank, gru_bias.reshape(1, -1), memory, agg, gh, held, gru_in)


def solution(mesh):
    sizes = (mesh.shape["node"] * mesh.shape["tm"], mesh.shape["tm"])
    split = P(("node", "tm"))
    return jax.shard_map(
        functools.partial(on_device, sizes),
        mesh=mesh,
        in_specs=(split,) * 5 + (P(),) * 7,
        out_specs=split,
        check_vma=False,
    )
```

```python
import functools

import jax
import jax.numpy as jnp
from jax import lax
from jax.experimental import pallas as pl
from jax.experimental.pallas import tpu as pltpu
from jax.sharding import PartitionSpec as P

BF = jnp.bfloat16
F32 = jnp.float32
I32 = jnp.int32
QUARTERS = 4
FIELDS = 8
TILE = 256
HALVES = 2


def div(x, n):
    if n & (n - 1) == 0:
        return lax.shift_right_logical(x, jnp.full_like(x, n.bit_length() - 1))
    return lax.div(x, jnp.full_like(x, n))


def rem(x, n):
    if n & (n - 1) == 0:
        return lax.bitwise_and(x, jnp.full_like(x, n - 1))
    return lax.rem(x, jnp.full_like(x, n))


def iota(rows, columns, axis):
    return lax.broadcasted_iota(I32, (rows, columns), axis)


def ones_where(condition):
    return jnp.where(condition, 1.0, 0.0).astype(BF)


def dot(a, b):
    return jnp.dot(a, b, preferred_element_type=F32)


def to_column(row):
    n = row.shape[1]
    return jnp.sum(jnp.where(iota(n, n, 0) == iota(n, n, 1), row, 0.0), axis=1, keepdims=True)


def to_row(column):
    n = column.shape[0]
    return jnp.sum(jnp.where(iota(n, n, 0) == iota(n, n, 1), column, 0.0), axis=0, keepdims=True)


def kernel(
    cfg,
    owner_hbm, row_hbm, mask_hbm, feat_hbm, b1_hbm, b2_hbm,
    mem_hbm, w1_hbm, w2_hbm, wh_hbm,
    agg_out, gh_out, held_out, rank_out, total_out,
    agg, held, rank, total_rows,
    owner_ref, row_ref, mask_ref, feat_ref, b1_ref, b2_ref,
    mem, w1, w2, wh, gh, table_out, table_in, fetched, acc, hidden, tally,
    main_row, main_flag, tail_row, tail_flag, tail_acc, sums,
    ans_main, ret_main, msg_main, inc_main, ans_tail, ret_tail, msg_tail, inc_tail,
    load_sem, send_sem, recv_sem, own_sem, store_sem,
):
    D, tm, m, R = cfg
    N, DM = mem.shape
    E = owner_ref.shape[1]
    HID = hidden.shape[1]
    QW = DM // QUARTERS
    HW = DM // HALVES
    tr = QUARTERS * R
    ranks = agg_out.shape[0]
    me = lax.axis_index("node") * tm + lax.axis_index("tm")

    loads = []
    for i, (src, dst) in enumerate(
        (
            (owner_hbm, owner_ref), (row_hbm, row_ref), (mask_hbm, mask_ref),
            (mem_hbm, mem), (wh_hbm, wh), (w1_hbm, w1), (w2_hbm, w2),
            (feat_hbm, feat_ref), (b1_hbm, b1_ref), (b2_hbm, b2_ref),
        )
    ):
        c = pltpu.make_async_copy(src, dst, load_sem.at[i])
        c.start()
        loads.append(c)

    barrier = pltpu.get_barrier_semaphore()

    @pl.loop(1, D)
    def _(i):
        peer = lax.rem(me + i, D)
        pl.semaphore_signal(
            barrier, inc=1, device_id=(peer // tm, lax.rem(peer, tm)),
            device_id_type=pl.DeviceIdType.MESH,
        )

    def start_exchange(k, pieces):
        for n, (src, dst, rows) in enumerate(pieces):
            pltpu.make_async_copy(
                src.at[pl.ds(pl.multiple_of(me * rows, rows), rows)],
                dst.at[pl.ds(pl.multiple_of(me * rows, rows), rows)],
                own_sem.at[k + n],
            ).start()

        @pl.loop(1, D)
        def _(i):
            peer = lax.rem(me + i, D)
            for n, (src, dst, rows) in enumerate(pieces):
                pltpu.make_async_remote_copy(
                    src_ref=src.at[pl.ds(pl.multiple_of(peer * rows, rows), rows)],
                    dst_ref=dst.at[pl.ds(pl.multiple_of(me * rows, rows), rows)],
                    send_sem=send_sem.at[k + n],
                    recv_sem=recv_sem.at[k + n],
                    device_id=(peer // tm, lax.rem(peer, tm)),
                    device_id_type=pl.DeviceIdType.MESH,
                ).start()

    def wait_received(k, pieces):
        for n, (src, dst, rows) in enumerate(pieces):
            part = dst.at[pl.ds(0, (D - 1) * rows)]
            pltpu.make_async_copy(part, part, recv_sem.at[k + n]).wait()
            own = dst.at[pl.ds(0, rows)]
            pltpu.make_async_copy(own, own, own_sem.at[k + n]).wait()

    def wait_sent(k, pieces):
        for n, (src, dst, rows) in enumerate(pieces):
            part = src.at[pl.ds(0, (D - 1) * rows)]
            pltpu.make_async_copy(part, part, send_sem.at[k + n]).wait()

    tables = [(table_out, table_in, FIELDS)]
    ans_t = [(ans_tail, ret_tail, tr)]
    msg_t = [(msg_tail, inc_tail, tr)]
    ans_m = [[(ans_main.at[h], ret_main.at[h], m)] if m else [] for h in range(HALVES)]
    msg_m = [[(msg_main.at[h], inc_main.at[h], m)] if m else [] for h in range(HALVES)]

    for c in loads[:3]:
        c.wait()

    owner = jnp.concatenate([owner_ref[0:1, :], owner_ref[1:2, :]], axis=1)
    wanted = jnp.concatenate([row_ref[0:1, :], row_ref[1:2, :]], axis=1)
    flag = jnp.concatenate([jnp.zeros((1, E), I32), mask_ref[...]], axis=1)
    onehot = jnp.where(iota(D, 2 * E, 0) == owner, 1.0, 0.0)
    earlier = ones_where(iota(2 * E, 2 * E, 0) < iota(2 * E, 2 * E, 1))
    position = jnp.sum(onehot * dot(onehot.astype(BF), earlier), axis=0, keepdims=True).astype(I32)
    field = rem(iota(D * FIELDS, 2 * E, 0), FIELDS)
    value = jnp.where(
        field == 0, div(wanted, 32) + 1,
        jnp.where(field == 1, rem(wanted, 32), jnp.where(field == 2, flag, 0)),
    )
    value = jnp.where(div(iota(D * FIELDS, 2 * E, 0), FIELDS) == owner, value, 0)
    place = ones_where(iota(128, 2 * E, 0) == position)
    table_out[...] = lax.dot_general(
        value.astype(F32).astype(BF), place, (((1,), (1,)), ((), ())), preferred_element_type=F32
    )
    pl.semaphore_wait(barrier, D - 1)
    start_exchange(0, tables)

    far = -4 * D * (m + tr)
    at_main = jnp.where(position < m, owner * m + position, far)
    at_tail = jnp.where(position >= m, owner * tr + position - m, far)
    main_column = to_column(at_main.astype(F32)).astype(I32)
    tail_column = to_column(at_tail.astype(F32)).astype(I32)
    sent_main = jnp.where(flag[:, E:] > 0, at_main[:, E:], far)
    sent_tail = jnp.where(flag[:, E:] > 0, at_tail[:, E:], far)

    loads[3].wait()
    wait_received(0, tables)

    table = table_in[...].astype(BF)

    def slots(base, size, block, first, period):
        s = base + iota(size, D * FIELDS, 0)
        field_row = iota(size, D * FIELDS, 1)
        start = div(s, block) * FIELDS
        pick = jnp.where(field_row == start, 32.0, jnp.where(field_row == start + 1, 1.0, 0.0))
        lane = iota(size, 128, 1) == first + rem(base + iota(size, 128, 0), period)
        ids = jnp.sum(jnp.where(lane, dot(pick.astype(BF), table), 0.0), axis=1, keepdims=True)
        marks = jnp.sum(
            jnp.where(lane, dot(ones_where(field_row == start + 2), table), 0.0),
            axis=1, keepdims=True,
        )
        return ids - 32.0, marks

    chunk = min(512, D * tr)

    @pl.loop(0, D * tr // chunk)
    def _(step):
        base = pl.multiple_of(step * chunk, chunk)
        ids, marks = slots(base, chunk, tr, m, R)
        quarter = rem(div(base + iota(chunk, 1, 0), R), QUARTERS)
        tail_row[:, pl.ds(base, chunk)] = to_row(ids).astype(I32)
        tail_flag[:, pl.ds(base, chunk)] = to_row(jnp.where(quarter == 0, marks, 0.0))
        total = jnp.zeros((chunk, QW), F32)
        nodes = iota(chunk, N, 1)
        for q in range(QUARTERS):
            hit = ones_where(nodes == jnp.where(quarter == q, ids.astype(I32), -1))
            total = total + dot(hit, mem[:, q * QW : (q + 1) * QW])
        ans_tail[pl.ds(base, chunk), :] = total.astype(BF)

    start_exchange(1, ans_t)

    if m:
        main_chunk = min(512, D * m)
        main_steps = D * m // main_chunk
        for h in range(HALVES):

            @pl.loop(0, main_steps)
            def _(step):
                base = pl.multiple_of(step * main_chunk, main_chunk)
                ids, marks = slots(base, main_chunk, m, 0, m)
                if h == 0:
                    main_row[:, pl.ds(base, main_chunk)] = to_row(ids).astype(I32)
                    main_flag[:, pl.ds(base, main_chunk)] = to_row(marks)
                hit = ones_where(iota(main_chunk, N, 1) == ids.astype(I32))
                ans_main[h, pl.ds(base, main_chunk), :] = dot(
                    hit, mem[:, h * HW : (h + 1) * HW]
                ).astype(BF)

            start_exchange(2 + h, ans_m[h])

    @pl.loop(0, N // TILE)
    def _(t):
        base = pl.multiple_of(t * TILE, TILE)
        nodes = base + iota(TILE, D * tr, 0)
        count = jnp.sum(jnp.where(tail_row[...] == nodes, tail_flag[...], 0.0), axis=1, keepdims=True)
        if m:
            nodes = base + iota(TILE, D * m, 0)
            count = count + jnp.sum(
                jnp.where(main_row[...] == nodes, main_flag[...], 0.0), axis=1, keepdims=True
            )
        tally[pl.ds(base, TILE), :] = count

    tally_row = to_row(tally[...])
    touched_row = jnp.where(tally_row > 0.5, 1.0, 0.0)
    earlier = ones_where(iota(N, N, 0) < iota(N, N, 1))
    before = dot(jnp.broadcast_to(touched_row, (8, N)).astype(BF), earlier)[0:1, :]
    rank_row = jnp.where(touched_row > 0.5, before, -1.0)
    rank_column = to_column(rank_row)
    rank[...] = jnp.broadcast_to(rank_column, (N, 128)).astype(I32)
    total_rows[...] = jnp.broadcast_to(
        jnp.sum(touched_row, axis=1, keepdims=True), (8, 128)
    ).astype(I32)

    def rank_slots(row_ref, count, size):
        @pl.loop(0, count // size)
        def _(step):
            cols = pl.ds(pl.multiple_of(step * size, size), size)
            same = iota(N, size, 0) == row_ref[:, cols]
            row_ref[:, cols] = jnp.sum(
                jnp.where(same, rank_column, 0.0), axis=0, keepdims=True
            ).astype(I32)

    rank_slots(tail_row, D * tr, chunk)
    if m:
        rank_slots(main_row, D * m, main_chunk)

    loads[4].wait()

    @pl.loop(0, ranks // TILE)
    def _(t):
        base = pl.multiple_of(t * TILE, TILE)
        rows = pl.ds(base, TILE)
        pick = rank_row.astype(I32) == base + iota(TILE, N, 0)
        tally[rows, :] = jnp.sum(jnp.where(pick, tally_row, 0.0), axis=1, keepdims=True)
        pick = ones_where(pick)

        @pl.loop(0, DM // TILE)
        def _(c):
            cols = pl.ds(pl.multiple_of(c * TILE, TILE), TILE)
            held[rows, cols] = dot(pick, mem[:, cols]).astype(BF)

    @pl.loop(0, 3 * DM // TILE)
    def _(t):
        cols = pl.ds(pl.multiple_of(t * TILE, TILE), TILE)
        gh[:, cols] = dot(held[...], wh[:, cols])

    stores = []
    for i, (src, dst) in enumerate(
        ((gh, gh_out), (held, held_out), (rank, rank_out), (total_rows, total_out))
    ):
        c = pltpu.make_async_copy(src, dst, store_sem.at[i])
        c.start()
        stores.append(c)

    for c in loads[5:]:
        c.wait()
    feat_width = feat_ref.shape[1]

    @pl.loop(0, HID // TILE)
    def _(t):
        cols = pl.ds(pl.multiple_of(t * TILE, TILE), TILE)
        acc[:, cols] = dot(feat_ref[...], w1[2 * DM : 2 * DM + feat_width, cols]) + b1_ref[:, cols]

    wait_received(1, ans_t)
    if m:
        from_main = ones_where(iota(2 * E, D * m, 1) == main_column)

    for h in range(HALVES):
        wait_received(2 + h, ans_m[h])
        got = []
        for q in range(h * QUARTERS // HALVES, (h + 1) * QUARTERS // HALVES):
            got.append(dot(ones_where(iota(2 * E, D * tr, 1) == tail_column + q * R), ret_tail[...]))
        got = jnp.concatenate(got, axis=1)
        if m:
            got = got + dot(from_main, ret_main[h])
        fetched[...] = got.astype(BF)

        @pl.loop(0, HID // TILE)
        def _(t):
            cols = pl.ds(pl.multiple_of(t * TILE, TILE), TILE)
            total = acc[:, cols] + dot(fetched[0:E, :], w1[h * HW : (h + 1) * HW, cols])
            total = total + dot(fetched[E : 2 * E, :], w1[DM + h * HW : DM + (h + 1) * HW, cols])
            if h == HALVES - 1:
                hidden[:, cols] = jnp.maximum(total, 0.0).astype(BF)
            else:
                acc[:, cols] = total

    tail_acc[...] = jnp.zeros_like(tail_acc)
    if m:
        to_main = ones_where(iota(D * m, E, 0) == sent_main)
    k = 2 + HALVES
    for h in range(HALVES):
        cols = slice(h * HW, (h + 1) * HW)
        message = (dot(hidden[...], w2[:, cols]) + b2_ref[:, cols]).astype(BF)
        if m:
            msg_main[h] = dot(to_main, message).astype(BF)
            start_exchange(k + 1 + h, msg_m[h])
        for j in range(QUARTERS // HALVES):
            q = h * QUARTERS // HALVES + j
            tail_acc[...] += dot(
                ones_where(iota(D * tr, E, 0) == sent_tail + q * R),
                message[:, j * QW : (j + 1) * QW],
            )

    msg_tail[...] = tail_acc[...].astype(BF)
    start_exchange(k, msg_t)
    wait_sent(0, tables)
    wait_sent(1, ans_t)
    for h in range(HALVES):
        wait_sent(2 + h, ans_m[h])
    for c in stores:
        c.wait()

    quarter = rem(div(iota(1, D * tr, 1), R), QUARTERS)
    for h in range(HALVES):
        wait_received(k + 1 + h, msg_m[h])
        if h == HALVES - 1:
            wait_received(k, msg_t)
        if m:

            @pl.loop(0, ranks // TILE)
            def _(t):
                base = pl.multiple_of(t * TILE, TILE)
                rows = pl.ds(base, TILE)
                hit = ones_where(main_row[...] == base + iota(TILE, D * m, 0))
                sums[rows, h * HW : (h + 1) * HW] = dot(hit, inc_main[h])

    @pl.loop(0, ranks // TILE)
    def _(t):
        base = pl.multiple_of(t * TILE, TILE)
        rows = pl.ds(base, TILE)
        count = jnp.maximum(tally[rows, :], 1.0)
        for q in range(QUARTERS):
            cols = slice(q * QW, (q + 1) * QW)
            wanted_rank = base + iota(TILE, D * tr, 0)
            hit = ones_where(jnp.where(quarter == q, tail_row[...], -1) == wanted_rank)
            summed = dot(hit, inc_tail[...])
            if m:
                summed = summed + sums[rows, cols]
            agg[rows, cols] = (summed / count).astype(BF)
        pltpu.make_async_copy(agg.at[rows], agg_out.at[rows], store_sem.at[len(stores)]).start()

    pltpu.make_async_copy(agg, agg_out, store_sem.at[len(stores)]).wait()
    wait_sent(k, msg_t)
    for h in range(HALVES):
        wait_sent(k + 1 + h, msg_m[h])


def gru_kernel(
    total_ref, rank_hbm, gb_hbm, mem_hbm, agg_hbm, held_hbm, wi_hbm, gh_hbm,
    out_hbm,
    rank_ref, gb_ref, mem, agg, held, wi, gh, fresh, out,
    small_sem, tile_sem, weight_sem, gate_sem, mem_sem, out_sem,
):
    N, DM = mem.shape
    steps = DM // TILE
    tiles = lax.div(total_ref[0, 0] + (TILE - 1), TILE)

    def columns(c, gate=0):
        return slice(gate * DM + c * TILE, gate * DM + (c + 1) * TILE)

    def tile_copies(base):
        rows = pl.ds(base, TILE)
        return [
            pltpu.make_async_copy(agg_hbm.at[rows], agg, tile_sem.at[0]),
            pltpu.make_async_copy(held_hbm.at[rows], held, tile_sem.at[1]),
        ]

    def gate_copies(base, c):
        return [
            pltpu.make_async_copy(
                gh_hbm.at[pl.ds(base, TILE), columns(c, g)], gh.at[:, columns(c, g)],
                gate_sem.at[c, g],
            )
            for g in range(3)
        ]

    def weight_copies(c):
        return [
            pltpu.make_async_copy(
                wi_hbm.at[:, columns(c, g)], wi.at[:, columns(c, g)], weight_sem.at[c, g]
            )
            for g in range(3)
        ]

    def mem_copy(c):
        return pltpu.make_async_copy(
            mem_hbm.at[:, columns(c)], mem.at[:, columns(c)], mem_sem.at[c]
        )

    def out_copy(c):
        return pltpu.make_async_copy(
            out.at[:, columns(c)], out_hbm.at[:, columns(c)], out_sem.at[c]
        )

    small = [
        pltpu.make_async_copy(gb_hbm, gb_ref, small_sem.at[0]),
        pltpu.make_async_copy(rank_hbm, rank_ref, small_sem.at[1]),
    ]

    def tile(t):
        first = isinstance(t, int)
        base = t * TILE if first else pl.multiple_of(t * TILE, TILE)
        for c in tile_copies(base):
            c.start()
        for c in range(steps):
            if first:
                for copy in weight_copies(c):
                    copy.start()
                if c == 0:
                    for copy in small:
                        copy.start()
            for copy in gate_copies(base, c):
                copy.start()
            if first:
                mem_copy(c).start()
        for c in tile_copies(base):
            c.wait()
        if first:
            for copy in small:
                copy.wait()
        column = rank_ref[:, 0:1] - base
        place = ones_where(column == iota(N, TILE, 1))
        mine = (column >= 0) & (column < TILE)
        for c in range(steps):
            if first:
                for copy in weight_copies(c):
                    copy.wait()
            gates = [
                dot(agg[...], wi[:, columns(c, g)]) + gb_ref[:, columns(c, g)] for g in range(3)
            ]
            for copy in gate_copies(base, c):
                copy.wait()
            reset = 0.5 * jnp.tanh(0.5 * (gates[0] + gh[:, columns(c, 0)])) + 0.5
            update = 0.5 * jnp.tanh(0.5 * (gates[1] + gh[:, columns(c, 1)])) + 0.5
            candidate = jnp.tanh(gates[2] + reset * gh[:, columns(c, 2)])
            previous = held[:, columns(c)].astype(F32)
            fresh[:, columns(c)] = ((1.0 - update) * candidate + update * previous).astype(BF)
            moved = dot(place, fresh[:, columns(c)])
            if first:
                mem_copy(c).wait()
            before = mem[:, columns(c)] if first else out[:, columns(c)]
            out[:, columns(c)] = jnp.where(mine, moved, before.astype(F32)).astype(BF)

            @pl.when(tiles <= 1 if first else t == tiles - 1)
            def _():
                out_copy(c).start()

    tile(0)

    @pl.loop(1, tiles)
    def _(t):
        tile(t)

    for c in range(steps):
        out_copy(c).wait()


def on_device(
    mesh_sizes,
    memory,
    ends_owner,
    ends_row,
    event_mask,
    edge_feat,
    msg_w1,
    msg_b1,
    msg_w2,
    msg_b2,
    gru_in,
    gru_hid,
    gru_bias,
):
    D, tm = mesh_sizes
    E = ends_owner.shape[0]
    N, DM = memory.shape
    HID = msg_w2.shape[0]
    cap = 5 * E // (2 * D)
    m = cap // 16 * 16
    R = max(4, -(-(cap - m) // 4) * 4)
    tr = QUARTERS * R
    QW = DM // QUARTERS
    mains = D * m if m else 16
    ranks = -(-min(N, D * cap) // TILE) * TILE
    smem = pl.BlockSpec(memory_space=pltpu.SMEM)
    hbm = pl.BlockSpec(memory_space=pltpu.HBM)
    phases = 3 + 2 * HALVES
    agg, gh, held, rank, total = pl.pallas_call(
        functools.partial(kernel, (D, tm, m, R)),
        out_shape=[
            jax.ShapeDtypeStruct((ranks, DM), BF),
            jax.ShapeDtypeStruct((ranks, 3 * DM), F32),
            jax.ShapeDtypeStruct((ranks, DM), BF),
            jax.ShapeDtypeStruct((N, 128), I32),
            jax.ShapeDtypeStruct((8, 128), I32),
        ],
        in_specs=[hbm] * 10,
        out_specs=[hbm] * 5,
        scratch_shapes=[
            pltpu.VMEM((ranks, DM), BF),
            pltpu.VMEM((ranks, DM), BF),
            pltpu.VMEM((N, 128), I32),
            pltpu.VMEM((8, 128), I32),
            pltpu.VMEM((2, E), I32),
            pltpu.VMEM((2, E), I32),
            pltpu.VMEM((1, E), I32),
            pltpu.VMEM(edge_feat.shape, BF),
            pltpu.VMEM((1, HID), F32),
            pltpu.VMEM((1, DM), F32),
            pltpu.VMEM(memory.shape, BF),
            pltpu.VMEM(msg_w1.shape, BF),
            pltpu.VMEM(msg_w2.shape, BF),
            pltpu.VMEM(gru_hid.shape, BF),
            pltpu.VMEM((ranks, 3 * DM), F32),
            pltpu.VMEM((D * FIELDS, 128), F32),
            pltpu.VMEM((D * FIELDS, 128), F32),
            pltpu.VMEM((2 * E, DM // HALVES), BF),
            pltpu.VMEM((E, HID), F32),
            pltpu.VMEM((E, HID), BF),
            pltpu.VMEM((N, 1), F32),
            pltpu.VMEM((1, mains), I32),
            pltpu.VMEM((1, mains), F32),
            pltpu.VMEM((1, D * tr), I32),
            pltpu.VMEM((1, D * tr), F32),
            pltpu.VMEM((D * tr, QW), F32),
            pltpu.VMEM((ranks, DM), F32),
        ]
        + [pltpu.VMEM((HALVES, mains, DM // HALVES), BF)] * 4
        + [pltpu.VMEM((D * tr, QW), BF)] * 4
        + [
            pltpu.SemaphoreType.DMA((10,)),
            pltpu.SemaphoreType.DMA((phases,)),
            pltpu.SemaphoreType.DMA((phases,)),
            pltpu.SemaphoreType.DMA((phases,)),
            pltpu.SemaphoreType.DMA((5,)),
        ],
        compiler_params=pltpu.CompilerParams(
            collective_id=0, has_side_effects=True, vmem_limit_bytes=60 * 2**20
        ),
    )(
        ends_owner.T,
        ends_row.T,
        event_mask.reshape(1, E),
        edge_feat,
        msg_b1.reshape(1, -1),
        msg_b2.reshape(1, -1),
        memory,
        msg_w1,
        msg_w2,
        gru_hid,
    )
    return pl.pallas_call(
        gru_kernel,
        out_shape=jax.ShapeDtypeStruct((N, DM), BF),
        in_specs=[smem] + [hbm] * 7,
        out_specs=hbm,
        scratch_shapes=[
            pltpu.VMEM((N, 128), I32),
            pltpu.VMEM((1, 3 * DM), F32),
            pltpu.VMEM((N, DM), BF),
            pltpu.VMEM((TILE, DM), BF),
            pltpu.VMEM((TILE, DM), BF),
            pltpu.VMEM(gru_in.shape, BF),
            pltpu.VMEM((TILE, 3 * DM), F32),
            pltpu.VMEM((TILE, DM), BF),
            pltpu.VMEM((N, DM), BF),
            pltpu.SemaphoreType.DMA((2,)),
            pltpu.SemaphoreType.DMA((2,)),
            pltpu.SemaphoreType.DMA((DM // TILE, 3)),
            pltpu.SemaphoreType.DMA((DM // TILE, 3)),
            pltpu.SemaphoreType.DMA((DM // TILE,)),
            pltpu.SemaphoreType.DMA((DM // TILE,)),
        ],
        compiler_params=pltpu.CompilerParams(vmem_limit_bytes=60 * 2**20),
    )(total, rank, gru_bias.reshape(1, -1), memory, agg, held, gru_in, gh)


def solution(mesh):
    sizes = (mesh.shape["node"] * mesh.shape["tm"], mesh.shape["tm"])
    split = P(("node", "tm"))
    return jax.shard_map(
        functools.partial(on_device, sizes),
        mesh=mesh,
        in_specs=(split,) * 5 + (P(),) * 7,
        out_specs=split,
        check_vma=False,
    )
```

```python
import functools

import jax
import jax.numpy as jnp
from jax import lax
from jax.experimental import pallas as pl
from jax.experimental.pallas import tpu as pltpu
from jax.sharding import PartitionSpec as P

BF = jnp.bfloat16
F32 = jnp.float32
I32 = jnp.int32
QUARTERS = 4
FIELDS = 8
TILE = 256
HALVES = 2


def div(x, n):
    if n & (n - 1) == 0:
        return lax.shift_right_logical(x, jnp.full_like(x, n.bit_length() - 1))
    return lax.div(x, jnp.full_like(x, n))


def rem(x, n):
    if n & (n - 1) == 0:
        return lax.bitwise_and(x, jnp.full_like(x, n - 1))
    return lax.rem(x, jnp.full_like(x, n))


def iota(rows, columns, axis):
    return lax.broadcasted_iota(I32, (rows, columns), axis)


def ones_where(condition):
    return jnp.where(condition, 1.0, 0.0).astype(BF)


def dot(a, b):
    return jnp.dot(a, b, preferred_element_type=F32)


def to_column(row):
    n = row.shape[1]
    return jnp.sum(jnp.where(iota(n, n, 0) == iota(n, n, 1), row, 0.0), axis=1, keepdims=True)


def to_row(column):
    n = column.shape[0]
    return jnp.sum(jnp.where(iota(n, n, 0) == iota(n, n, 1), column, 0.0), axis=0, keepdims=True)


def kernel(
    cfg,
    owner_hbm, row_hbm, mask_hbm, feat_hbm, b1_hbm, b2_hbm,
    mem_hbm, w1_hbm, w2_hbm, wh_hbm, wi_hbm, gb_hbm,
    agg_out, gh_out, held_out, rank_out, total_out, fresh_out,
    agg, held, rank, total_rows, fresh, wi, gb_ref, from_tail, sum_main, sum_tail,
    owner_ref, row_ref, mask_ref, feat_ref, b1_ref, b2_ref,
    mem, w1, w2, wh, gh, table_out, table_in, fetched, acc, hidden, tally,
    main_row, main_flag, tail_row, tail_flag, sums,
    ans_main, ret_main, msg_main, inc_main, ans_tail, ret_tail, msg_tail, inc_tail,
    load_sem, send_sem, recv_sem, own_sem, store_sem,
):
    D, tm, m, R = cfg
    N, DM = mem.shape
    E = owner_ref.shape[1]
    HID = hidden.shape[1]
    QW = DM // QUARTERS
    HW = DM // HALVES
    tr = QUARTERS * R
    ranks = agg_out.shape[0]
    me = lax.axis_index("node") * tm + lax.axis_index("tm")

    loads = []
    for i, (src, dst) in enumerate(
        (
            (owner_hbm, owner_ref), (row_hbm, row_ref), (mask_hbm, mask_ref),
            (mem_hbm, mem), (wh_hbm, wh), (w1_hbm, w1), (w2_hbm, w2),
            (feat_hbm, feat_ref), (b1_hbm, b1_ref), (b2_hbm, b2_ref),
            (wi_hbm, wi), (gb_hbm, gb_ref),
        )
    ):
        c = pltpu.make_async_copy(src, dst, load_sem.at[i])
        c.start()
        loads.append(c)

    barrier = pltpu.get_barrier_semaphore()

    @pl.loop(1, D)
    def _(i):
        peer = lax.rem(me + i, D)
        pl.semaphore_signal(
            barrier, inc=1, device_id=(peer // tm, lax.rem(peer, tm)),
            device_id_type=pl.DeviceIdType.MESH,
        )

    def start_exchange(k, pieces):
        for n, (src, dst, rows) in enumerate(pieces):
            pltpu.make_async_copy(
                src.at[pl.ds(pl.multiple_of(me * rows, rows), rows)],
                dst.at[pl.ds(pl.multiple_of(me * rows, rows), rows)],
                own_sem.at[k + n],
            ).start()

        @pl.loop(1, D)
        def _(i):
            peer = lax.rem(me + i, D)
            for n, (src, dst, rows) in enumerate(pieces):
                pltpu.make_async_remote_copy(
                    src_ref=src.at[pl.ds(pl.multiple_of(peer * rows, rows), rows)],
                    dst_ref=dst.at[pl.ds(pl.multiple_of(me * rows, rows), rows)],
                    send_sem=send_sem.at[k + n],
                    recv_sem=recv_sem.at[k + n],
                    device_id=(peer // tm, lax.rem(peer, tm)),
                    device_id_type=pl.DeviceIdType.MESH,
                ).start()

    def wait_received(k, pieces):
        for n, (src, dst, rows) in enumerate(pieces):
            part = dst.at[pl.ds(0, (D - 1) * rows)]
            pltpu.make_async_copy(part, part, recv_sem.at[k + n]).wait()
            own = dst.at[pl.ds(0, rows)]
            pltpu.make_async_copy(own, own, own_sem.at[k + n]).wait()

    def wait_sent(k, pieces):
        for n, (src, dst, rows) in enumerate(pieces):
            part = src.at[pl.ds(0, (D - 1) * rows)]
            pltpu.make_async_copy(part, part, send_sem.at[k + n]).wait()

    tables = [(table_out, table_in, FIELDS)]
    ans_t = [(ans_tail, ret_tail, tr)]
    msg_t = [(msg_tail, inc_tail, tr)]
    ans_m = [[(ans_main.at[h], ret_main.at[h], m)] if m else [] for h in range(HALVES)]
    msg_m = [[(msg_main.at[h], inc_main.at[h], m)] if m else [] for h in range(HALVES)]

    for c in loads[:3]:
        c.wait()

    owner = jnp.concatenate([owner_ref[0:1, :], owner_ref[1:2, :]], axis=1)
    wanted = jnp.concatenate([row_ref[0:1, :], row_ref[1:2, :]], axis=1)
    flag = jnp.concatenate([jnp.zeros((1, E), I32), mask_ref[...]], axis=1)
    onehot = jnp.where(iota(D, 2 * E, 0) == owner, 1.0, 0.0)
    earlier = ones_where(iota(2 * E, 2 * E, 0) < iota(2 * E, 2 * E, 1))
    position = jnp.sum(onehot * dot(onehot.astype(BF), earlier), axis=0, keepdims=True).astype(I32)
    field = rem(iota(D * FIELDS, 2 * E, 0), FIELDS)
    value = jnp.where(
        field == 0, div(wanted, 32) + 1,
        jnp.where(field == 1, rem(wanted, 32), jnp.where(field == 2, flag, 0)),
    )
    value = jnp.where(div(iota(D * FIELDS, 2 * E, 0), FIELDS) == owner, value, 0)
    place = ones_where(iota(128, 2 * E, 0) == position)
    table_out[...] = lax.dot_general(
        value.astype(F32).astype(BF), place, (((1,), (1,)), ((), ())), preferred_element_type=F32
    )
    pl.semaphore_wait(barrier, D - 1)
    start_exchange(0, tables)

    far = -4 * D * (m + tr)
    at_main = jnp.where(position < m, owner * m + position, far)
    at_tail = jnp.where(position >= m, owner * tr + position - m, far)
    main_column = to_column(at_main.astype(F32)).astype(I32)
    tail_column = to_column(at_tail.astype(F32)).astype(I32)
    sent_main = jnp.where(flag[:, E:] > 0, at_main[:, E:], far)
    sent_tail = jnp.where(flag[:, E:] > 0, at_tail[:, E:], far)

    loads[3].wait()
    wait_received(0, tables)

    table = table_in[...].astype(BF)

    def slots(base, size, block, first, period):
        s = base + iota(size, D * FIELDS, 0)
        field_row = iota(size, D * FIELDS, 1)
        start = div(s, block) * FIELDS
        pick = jnp.where(field_row == start, 32.0, jnp.where(field_row == start + 1, 1.0, 0.0))
        lane = iota(size, 128, 1) == first + rem(base + iota(size, 128, 0), period)
        ids = jnp.sum(jnp.where(lane, dot(pick.astype(BF), table), 0.0), axis=1, keepdims=True)
        marks = jnp.sum(
            jnp.where(lane, dot(ones_where(field_row == start + 2), table), 0.0),
            axis=1, keepdims=True,
        )
        return ids - 32.0, marks

    chunk = min(512, D * tr)
    main_chunk = min(512, D * m)

    def answer_main(h):
        @pl.loop(0, D * m // main_chunk)
        def _(step):
            base = pl.multiple_of(step * main_chunk, main_chunk)
            ids, marks = slots(base, main_chunk, m, 0, m)
            if h == 1:
                main_row[:, pl.ds(base, main_chunk)] = to_row(ids).astype(I32)
                main_flag[:, pl.ds(base, main_chunk)] = to_row(marks)
            hit = ones_where(iota(main_chunk, N, 1) == ids.astype(I32))
            ans_main[h, pl.ds(base, main_chunk), :] = dot(
                hit, mem[:, h * HW : (h + 1) * HW]
            ).astype(BF)

        start_exchange(2 + h, ans_m[h])

    if m:
        answer_main(0)

    @pl.loop(0, D * tr // chunk)
    def _(step):
        base = pl.multiple_of(step * chunk, chunk)
        ids, marks = slots(base, chunk, tr, m, R)
        quarter = rem(div(base + iota(chunk, 1, 0), R), QUARTERS)
        tail_row[:, pl.ds(base, chunk)] = to_row(ids).astype(I32)
        tail_flag[:, pl.ds(base, chunk)] = to_row(jnp.where(quarter == 0, marks, 0.0))
        total = jnp.zeros((chunk, QW), F32)
        hit = ones_where(iota(chunk, N, 1) == ids.astype(I32))
        for q in range(QUARTERS):
            total = total + jnp.where(quarter == q, dot(hit, mem[:, q * QW : (q + 1) * QW]), 0.0)
        ans_tail[pl.ds(base, chunk), :] = total.astype(BF)

    start_exchange(1, ans_t)
    if m:
        answer_main(1)

    @pl.loop(0, N // TILE)
    def _(t):
        base = pl.multiple_of(t * TILE, TILE)
        nodes = base + iota(TILE, D * tr, 0)
        count = jnp.sum(jnp.where(tail_row[...] == nodes, tail_flag[...], 0.0), axis=1, keepdims=True)
        if m:
            nodes = base + iota(TILE, D * m, 0)
            count = count + jnp.sum(
                jnp.where(main_row[...] == nodes, main_flag[...], 0.0), axis=1, keepdims=True
            )
        tally[pl.ds(base, TILE), :] = count

    tally_row = to_row(tally[...])
    touched_row = jnp.where(tally_row > 0.5, 1.0, 0.0)
    earlier = ones_where(iota(N, N, 0) < iota(N, N, 1))
    before = dot(jnp.broadcast_to(touched_row, (8, N)).astype(BF), earlier)[0:1, :]
    rank_row = jnp.where(touched_row > 0.5, before, -1.0)
    rank_column = to_column(rank_row)
    rank[...] = jnp.broadcast_to(rank_column, (N, 128)).astype(I32)
    total_rows[...] = jnp.broadcast_to(
        jnp.sum(touched_row, axis=1, keepdims=True), (8, 128)
    ).astype(I32)

    def rank_slots(row_ref, count, size):
        @pl.loop(0, count // size)
        def _(step):
            cols = pl.ds(pl.multiple_of(step * size, size), size)
            same = iota(N, size, 0) == row_ref[:, cols]
            row_ref[:, cols] = jnp.sum(
                jnp.where(same, rank_column, 0.0), axis=0, keepdims=True
            ).astype(I32)

    rank_slots(tail_row, D * tr, chunk)
    if m:
        rank_slots(main_row, D * m, main_chunk)

    loads[4].wait()

    @pl.loop(0, ranks // TILE)
    def _(t):
        base = pl.multiple_of(t * TILE, TILE)
        rows = pl.ds(base, TILE)
        pick = rank_row.astype(I32) == base + iota(TILE, N, 0)
        tally[rows, :] = jnp.sum(jnp.where(pick, tally_row, 0.0), axis=1, keepdims=True)
        pick = ones_where(pick)

        @pl.loop(0, DM // TILE)
        def _(c):
            cols = pl.ds(pl.multiple_of(c * TILE, TILE), TILE)
            held[rows, cols] = dot(pick, mem[:, cols]).astype(BF)

    @pl.loop(0, 3 * DM // TILE)
    def _(t):
        cols = pl.ds(pl.multiple_of(t * TILE, TILE), TILE)
        gh[:, cols] = dot(held[...], wh[:, cols])

    stores = []
    for i, (src, dst) in enumerate(
        ((gh, gh_out), (held, held_out), (rank, rank_out), (total_rows, total_out))
    ):
        c = pltpu.make_async_copy(src, dst, store_sem.at[i])
        c.start()
        stores.append(c)

    for c in loads[5:10]:
        c.wait()
    feat_width = feat_ref.shape[1]

    @pl.loop(0, HID // TILE)
    def _(t):
        cols = pl.ds(pl.multiple_of(t * TILE, TILE), TILE)
        acc[:, cols] = dot(feat_ref[...], w1[2 * DM : 2 * DM + feat_width, cols]) + b1_ref[:, cols]

    quarter_row = rem(div(iota(1, D * tr, 1), R), QUARTERS)
    quarter_column = rem(div(iota(D * tr, 1, 0), R), QUARTERS)
    lane = iota(1, D * tr, 1) - quarter_row * R
    from_tail[...] = ones_where(jnp.broadcast_to(lane, (2 * E, D * tr)) == tail_column)
    if m:
        from_main = ones_where(iota(2 * E, D * m, 1) == main_column)

    @pl.loop(0, ranks // TILE)
    def _(t):
        base = pl.multiple_of(t * TILE, TILE)
        rows = pl.ds(base, TILE)
        sum_tail[rows, :] = ones_where(tail_row[...] == base + iota(TILE, D * tr, 0))
        if m:
            sum_main[rows, :] = ones_where(main_row[...] == base + iota(TILE, D * m, 0))

    def of_quarter(ref, q):
        return ref[...] * ones_where(quarter_column == q)

    for h in range(HALVES):
        wait_received(2 + h, ans_m[h])
        if h == 0:
            wait_received(1, ans_t)
        got = []
        for q in range(h * QUARTERS // HALVES, (h + 1) * QUARTERS // HALVES):
            got.append(dot(from_tail[...], of_quarter(ret_tail, q)))
        got = jnp.concatenate(got, axis=1)
        if m:
            got = got + dot(from_main, ret_main[h])
        fetched[...] = got.astype(BF)

        @pl.loop(0, HID // TILE)
        def _(t):
            cols = pl.ds(pl.multiple_of(t * TILE, TILE), TILE)
            total = acc[:, cols] + dot(fetched[0:E, :], w1[h * HW : (h + 1) * HW, cols])
            total = total + dot(fetched[E : 2 * E, :], w1[DM + h * HW : DM + (h + 1) * HW, cols])
            if h == HALVES - 1:
                hidden[:, cols] = jnp.maximum(total, 0.0).astype(BF)
            else:
                acc[:, cols] = total

    to_tail = ones_where(iota(D * tr, E, 0) - quarter_column * R == sent_tail)
    if m:
        to_main = ones_where(iota(D * m, E, 0) == sent_main)
    k = 2 + HALVES
    for h in range(HALVES):
        cols = slice(h * HW, (h + 1) * HW)
        message = (dot(hidden[...], w2[:, cols]) + b2_ref[:, cols]).astype(BF)
        if m:
            msg_main[h] = dot(to_main, message).astype(BF)
            start_exchange(k + 1 + h, msg_m[h])
        moved = dot(to_tail, message)
        for j in range(QUARTERS // HALVES):
            part = jnp.where(
                quarter_column == h * QUARTERS // HALVES + j, moved[:, j * QW : (j + 1) * QW], 0.0
            ).astype(BF)
            msg_tail[...] = part if h == 0 and j == 0 else msg_tail[...] + part

    start_exchange(k, msg_t)
    wait_sent(0, tables)
    wait_sent(1, ans_t)
    for h in range(HALVES):
        wait_sent(2 + h, ans_m[h])
    for c in stores:
        c.wait()

    loads[10].wait()
    loads[11].wait()

    for h in range(HALVES):
        wait_received(k + 1 + h, msg_m[h])
        if m:

            @pl.loop(0, ranks // TILE)
            def _(t):
                rows = pl.ds(pl.multiple_of(t * TILE, TILE), TILE)
                sums[rows, h * HW : (h + 1) * HW] = dot(sum_main[rows, :], inc_main[h])

    wait_received(k, msg_t)
    for q in range(QUARTERS):
        cols = slice(q * QW, (q + 1) * QW)
        part = of_quarter(inc_tail, q)
        for t in range(ranks // TILE):
            rows = slice(t * TILE, (t + 1) * TILE)
            summed = dot(sum_tail[rows, :], part)
            if m:
                summed = summed + sums[rows, cols]
            agg[rows, cols] = (summed / jnp.maximum(tally[rows, :], 1.0)).astype(BF)
    last = pltpu.make_async_copy(agg, agg_out, store_sem.at[4])
    last.start()

    copies = []
    for c in range(DM // TILE):
        cols = slice(c * TILE, (c + 1) * TILE)
        fresh[:, cols] = gru_columns(agg[0:TILE, :], wi, gb_ref, gh, held, c)
        copy = pltpu.make_async_copy(fresh.at[:, cols], fresh_out.at[:, cols], store_sem.at[5 + c])
        copy.start()
        copies.append(copy)
    last.wait()
    for copy in copies:
        copy.wait()
    wait_sent(k, msg_t)
    for h in range(HALVES):
        wait_sent(k + 1 + h, msg_m[h])


def gru_columns(agg, wi, gb, gh, held, c):
    DM = agg.shape[1]
    gates, hid = [], []
    for g in range(3):
        part = slice(g * DM + c * TILE, g * DM + (c + 1) * TILE)
        gates.append(dot(agg, wi[:, part]) + gb[:, part])
        hid.append(gh[0:TILE, part])
    reset = 0.5 * jnp.tanh(0.5 * (gates[0] + hid[0])) + 0.5
    update = 0.5 * jnp.tanh(0.5 * (gates[1] + hid[1])) + 0.5
    candidate = jnp.tanh(gates[2] + reset * hid[2])
    previous = held[0:TILE, c * TILE : (c + 1) * TILE].astype(F32)
    return ((1.0 - update) * candidate + update * previous).astype(BF)


def place_kernel(
    total_ref, rank_hbm, gb_hbm, mem_hbm, agg_hbm, held_hbm, wi_hbm, gh_hbm, fresh_hbm,
    out_hbm,
    rank_ref, gb_ref, mem, agg, held, wi, gh, fresh, out,
    first_sem, tile_sem, mem_sem, out_sem,
):
    N, DM = mem.shape
    steps = DM // TILE
    tiles = lax.div(total_ref[0, 0] + (TILE - 1), TILE)

    def columns(c):
        return slice(c * TILE, (c + 1) * TILE)

    def mem_copy(c):
        return pltpu.make_async_copy(
            mem_hbm.at[:, columns(c)], mem.at[:, columns(c)], mem_sem.at[c]
        )

    def out_copy(c):
        return pltpu.make_async_copy(
            out.at[:, columns(c)], out_hbm.at[:, columns(c)], out_sem.at[c]
        )

    def place(base, c, before):
        column = rank_ref[:, 0:1] - base
        moved = dot(ones_where(column == iota(N, TILE, 1)), fresh[:, columns(c)])
        mine = (column >= 0) & (column < TILE)
        out[:, columns(c)] = jnp.where(mine, moved, before[:, columns(c)].astype(F32)).astype(BF)

    starts = [
        pltpu.make_async_copy(rank_hbm, rank_ref, first_sem.at[0]),
        pltpu.make_async_copy(fresh_hbm, fresh, first_sem.at[1]),
    ]
    for c in starts:
        c.start()
    for c in range(steps):
        mem_copy(c).start()
    for c in starts:
        c.wait()
    for c in range(steps):
        mem_copy(c).wait()
        place(0, c, mem)

        @pl.when(tiles <= 1)
        def _():
            out_copy(c).start()

    @pl.loop(1, tiles)
    def _(t):
        base = pl.multiple_of(t * TILE, TILE)
        rows = pl.ds(base, TILE)
        pairs = (
            (agg_hbm.at[rows], agg), (held_hbm.at[rows], held), (gh_hbm.at[rows], gh),
            (wi_hbm, wi), (gb_hbm, gb_ref),
        )
        copies = [pltpu.make_async_copy(a, b, tile_sem.at[i]) for i, (a, b) in enumerate(pairs)]
        for copy in copies:
            copy.start()
        for copy in copies:
            copy.wait()
        for c in range(steps):
            fresh[:, columns(c)] = gru_columns(agg[...], wi, gb_ref, gh, held, c)
            place(base, c, out)

            @pl.when(t == tiles - 1)
            def _():
                out_copy(c).start()

    for c in range(steps):
        out_copy(c).wait()


def on_device(
    mesh_sizes,
    memory,
    ends_owner,
    ends_row,
    event_mask,
    edge_feat,
    msg_w1,
    msg_b1,
    msg_w2,
    msg_b2,
    gru_in,
    gru_hid,
    gru_bias,
):
    D, tm = mesh_sizes
    E = ends_owner.shape[0]
    N, DM = memory.shape
    HID = msg_w2.shape[0]
    cap = 5 * E // (2 * D)
    m = cap // 16 * 16
    R = max(4, -(-(cap - m) // 4) * 4)
    tr = QUARTERS * R
    QW = DM // QUARTERS
    mains = D * m if m else 16
    ranks = -(-min(N, D * cap) // TILE) * TILE
    smem = pl.BlockSpec(memory_space=pltpu.SMEM)
    hbm = pl.BlockSpec(memory_space=pltpu.HBM)
    phases = 3 + 2 * HALVES
    agg, gh, held, rank, total, fresh = pl.pallas_call(
        functools.partial(kernel, (D, tm, m, R)),
        out_shape=[
            jax.ShapeDtypeStruct((ranks, DM), BF),
            jax.ShapeDtypeStruct((ranks, 3 * DM), F32),
            jax.ShapeDtypeStruct((ranks, DM), BF),
            jax.ShapeDtypeStruct((N, 128), I32),
            jax.ShapeDtypeStruct((8, 128), I32),
            jax.ShapeDtypeStruct((TILE, DM), BF),
        ],
        in_specs=[hbm] * 12,
        out_specs=[hbm] * 6,
        scratch_shapes=[
            pltpu.VMEM((ranks, DM), BF),
            pltpu.VMEM((ranks, DM), BF),
            pltpu.VMEM((N, 128), I32),
            pltpu.VMEM((8, 128), I32),
            pltpu.VMEM((TILE, DM), BF),
            pltpu.VMEM(gru_in.shape, BF),
            pltpu.VMEM((1, 3 * DM), F32),
            pltpu.VMEM((2 * E, D * tr), BF),
            pltpu.VMEM((ranks if m else 16, mains), BF),
            pltpu.VMEM((ranks, D * tr), BF),
            pltpu.VMEM((2, E), I32),
            pltpu.VMEM((2, E), I32),
            pltpu.VMEM((1, E), I32),
            pltpu.VMEM(edge_feat.shape, BF),
            pltpu.VMEM((1, HID), F32),
            pltpu.VMEM((1, DM), F32),
            pltpu.VMEM(memory.shape, BF),
            pltpu.VMEM(msg_w1.shape, BF),
            pltpu.VMEM(msg_w2.shape, BF),
            pltpu.VMEM(gru_hid.shape, BF),
            pltpu.VMEM((ranks, 3 * DM), F32),
            pltpu.VMEM((D * FIELDS, 128), F32),
            pltpu.VMEM((D * FIELDS, 128), F32),
            pltpu.VMEM((2 * E, DM // HALVES), BF),
            pltpu.VMEM((E, HID), F32),
            pltpu.VMEM((E, HID), BF),
            pltpu.VMEM((N, 1), F32),
            pltpu.VMEM((1, mains), I32),
            pltpu.VMEM((1, mains), F32),
            pltpu.VMEM((1, D * tr), I32),
            pltpu.VMEM((1, D * tr), F32),
            pltpu.VMEM((ranks if m else 8, DM), F32),
        ]
        + [pltpu.VMEM((HALVES, mains, DM // HALVES), BF)] * 4
        + [pltpu.VMEM((D * tr, QW), BF)] * 4
        + [
            pltpu.SemaphoreType.DMA((12,)),
            pltpu.SemaphoreType.DMA((phases,)),
            pltpu.SemaphoreType.DMA((phases,)),
            pltpu.SemaphoreType.DMA((phases,)),
            pltpu.SemaphoreType.DMA((5 + DM // TILE,)),
        ],
        compiler_params=pltpu.CompilerParams(
            collective_id=0, has_side_effects=True, vmem_limit_bytes=60 * 2**20
        ),
    )(
        ends_owner.T,
        ends_row.T,
        event_mask.reshape(1, E),
        edge_feat,
        msg_b1.reshape(1, -1),
        msg_b2.reshape(1, -1),
        memory,
        msg_w1,
        msg_w2,
        gru_hid,
        gru_in,
        gru_bias.reshape(1, -1),
    )
    return pl.pallas_call(
        place_kernel,
        out_shape=jax.ShapeDtypeStruct((N, DM), BF),
        in_specs=[smem] + [hbm] * 8,
        out_specs=hbm,
        scratch_shapes=[
            pltpu.VMEM((N, 128), I32),
            pltpu.VMEM((1, 3 * DM), F32),
            pltpu.VMEM((N, DM), BF),
            pltpu.VMEM((TILE, DM), BF),
            pltpu.VMEM((TILE, DM), BF),
            pltpu.VMEM(gru_in.shape, BF),
            pltpu.VMEM((TILE, 3 * DM), F32),
            pltpu.VMEM((TILE, DM), BF),
            pltpu.VMEM((N, DM), BF),
            pltpu.SemaphoreType.DMA((2,)),
            pltpu.SemaphoreType.DMA((5,)),
            pltpu.SemaphoreType.DMA((DM // TILE,)),
            pltpu.SemaphoreType.DMA((DM // TILE,)),
        ],
        compiler_params=pltpu.CompilerParams(vmem_limit_bytes=60 * 2**20),
    )(total, rank, gru_bias.reshape(1, -1), memory, agg, held, gru_in, gh, fresh)


def solution(mesh):
    sizes = (mesh.shape["node"] * mesh.shape["tm"], mesh.shape["tm"])
    split = P(("node", "tm"))
    return jax.shard_map(
        functools.partial(on_device, sizes),
        mesh=mesh,
        in_specs=(split,) * 5 + (P(),) * 7,
        out_specs=split,
        check_vma=False,
    )
```

```python
import functools

import jax
import jax.numpy as jnp
from jax import lax
from jax.experimental import pallas as pl
from jax.experimental.pallas import tpu as pltpu
from jax.sharding import PartitionSpec as P

BF = jnp.bfloat16
F32 = jnp.float32
I32 = jnp.int32
QUARTERS = 4
FIELDS = 8
TILE = 256
HALVES = 2


def div(x, n):
    if n & (n - 1) == 0:
        return lax.shift_right_logical(x, jnp.full_like(x, n.bit_length() - 1))
    return lax.div(x, jnp.full_like(x, n))


def rem(x, n):
    if n & (n - 1) == 0:
        return lax.bitwise_and(x, jnp.full_like(x, n - 1))
    return lax.rem(x, jnp.full_like(x, n))


def iota(rows, columns, axis):
    return lax.broadcasted_iota(I32, (rows, columns), axis)


def ones_where(condition):
    return jnp.where(condition, 1.0, 0.0).astype(BF)


def dot(a, b):
    return jnp.dot(a, b, preferred_element_type=F32)


def to_column(row):
    n = row.shape[1]
    return jnp.sum(jnp.where(iota(n, n, 0) == iota(n, n, 1), row, 0.0), axis=1, keepdims=True)


def to_row(column):
    n = column.shape[0]
    return jnp.sum(jnp.where(iota(n, n, 0) == iota(n, n, 1), column, 0.0), axis=0, keepdims=True)


def kernel(
    cfg,
    owner_hbm, row_hbm, mask_hbm, feat_hbm, b1_hbm, b2_hbm,
    mem_hbm, w1_hbm, w2_hbm, wh_hbm, wi_hbm, gb_hbm,
    agg_out, gh_out, held_out, rank_out, total_out, fresh_out,
    agg, held, rank, total_rows, fresh, wi, gb_ref, from_tail, sum_main, sum_tail,
    owner_ref, row_ref, mask_ref, feat_ref, b1_ref, b2_ref,
    mem, w1, w2, wh, gh, table_out, table_in, fetched, acc, hidden, tally,
    main_row, main_flag, tail_row, tail_flag, sums,
    ans_main, ret_main, msg_main, inc_main, ans_tail, ret_tail, msg_tail, inc_tail,
    load_sem, send_sem, recv_sem, own_sem, store_sem,
):
    D, tm, m, R = cfg
    N, DM = mem.shape
    E = owner_ref.shape[1]
    HID = hidden.shape[1]
    QW = DM // QUARTERS
    HW = DM // HALVES
    tr = QUARTERS * R
    ranks = agg_out.shape[0]
    nodes = D // tm
    me = lax.axis_index("node") * tm + lax.axis_index("tm")

    loads = []
    for i, (src, dst) in enumerate(
        (
            (owner_hbm, owner_ref), (row_hbm, row_ref), (mask_hbm, mask_ref),
            (mem_hbm, mem), (wh_hbm, wh), (w1_hbm, w1), (w2_hbm, w2),
            (feat_hbm, feat_ref), (b1_hbm, b1_ref), (b2_hbm, b2_ref),
            (wi_hbm, wi), (gb_hbm, gb_ref),
        )
    ):
        c = pltpu.make_async_copy(src, dst, load_sem.at[i])
        c.start()
        loads.append(c)

    barrier = pltpu.get_barrier_semaphore()

    @pl.loop(1, D)
    def _(i):
        peer = lax.rem(me + i, D)
        pl.semaphore_signal(
            barrier, inc=1, device_id=(peer // tm, lax.rem(peer, tm)),
            device_id_type=pl.DeviceIdType.MESH,
        )

    def start_exchange(k, pieces):
        for n, (src, dst, rows) in enumerate(pieces):
            pltpu.make_async_copy(
                src.at[pl.ds(pl.multiple_of(me * rows, rows), rows)],
                dst.at[pl.ds(pl.multiple_of(me * rows, rows), rows)],
                own_sem.at[k + n],
            ).start()

        @pl.loop(0, D - 1)
        def _(i):
            j = i // nodes
            away = (j + 1) // 2
            shift = tm // 2 + away - 2 * away * lax.rem(j + 1, 2)
            peer_node = lax.rem(lax.axis_index("node") + lax.rem(i, nodes) + 1, nodes)
            peer = peer_node * tm + lax.rem(lax.axis_index("tm") + shift, tm)
            for n, (src, dst, rows) in enumerate(pieces):
                pltpu.make_async_remote_copy(
                    src_ref=src.at[pl.ds(pl.multiple_of(peer * rows, rows), rows)],
                    dst_ref=dst.at[pl.ds(pl.multiple_of(me * rows, rows), rows)],
                    send_sem=send_sem.at[k + n],
                    recv_sem=recv_sem.at[k + n],
                    device_id=(peer // tm, lax.rem(peer, tm)),
                    device_id_type=pl.DeviceIdType.MESH,
                ).start()

    def wait_received(k, pieces):
        for n, (src, dst, rows) in enumerate(pieces):
            part = dst.at[pl.ds(0, (D - 1) * rows)]
            pltpu.make_async_copy(part, part, recv_sem.at[k + n]).wait()
            own = dst.at[pl.ds(0, rows)]
            pltpu.make_async_copy(own, own, own_sem.at[k + n]).wait()

    def wait_sent(k, pieces):
        for n, (src, dst, rows) in enumerate(pieces):
            part = src.at[pl.ds(0, (D - 1) * rows)]
            pltpu.make_async_copy(part, part, send_sem.at[k + n]).wait()

    tables = [(table_out, table_in, FIELDS)]
    ans_t = [(ans_tail, ret_tail, tr)]
    msg_t = [(msg_tail, inc_tail, tr)]
    ans_m = [[(ans_main.at[h], ret_main.at[h], m)] if m else [] for h in range(HALVES)]
    msg_m = [[(msg_main.at[h], inc_main.at[h], m)] if m else [] for h in range(HALVES)]

    for c in loads[:3]:
        c.wait()

    owner = jnp.concatenate([owner_ref[0:1, :], owner_ref[1:2, :]], axis=1)
    wanted = jnp.concatenate([row_ref[0:1, :], row_ref[1:2, :]], axis=1)
    flag = jnp.concatenate([jnp.zeros((1, E), I32), mask_ref[...]], axis=1)
    onehot = jnp.where(iota(D, 2 * E, 0) == owner, 1.0, 0.0)
    earlier = ones_where(iota(2 * E, 2 * E, 0) < iota(2 * E, 2 * E, 1))
    position = jnp.sum(onehot * dot(onehot.astype(BF), earlier), axis=0, keepdims=True).astype(I32)
    field = rem(iota(D * FIELDS, 2 * E, 0), FIELDS)
    value = jnp.where(
        field == 0, div(wanted, 32) + 1,
        jnp.where(field == 1, rem(wanted, 32), jnp.where(field == 2, flag, 0)),
    )
    value = jnp.where(div(iota(D * FIELDS, 2 * E, 0), FIELDS) == owner, value, 0)
    place = ones_where(iota(128, 2 * E, 0) == position)
    table_out[...] = lax.dot_general(
        value.astype(F32).astype(BF), place, (((1,), (1,)), ((), ())), preferred_element_type=F32
    )
    pl.semaphore_wait(barrier, D - 1)
    start_exchange(0, tables)

    far = -4 * D * (m + tr)
    at_main = jnp.where(position < m, owner * m + position, far)
    at_tail = jnp.where(position >= m, owner * tr + position - m, far)
    main_column = to_column(at_main.astype(F32)).astype(I32)
    tail_column = to_column(at_tail.astype(F32)).astype(I32)
    sent_main = jnp.where(flag[:, E:] > 0, at_main[:, E:], far)
    sent_tail = jnp.where(flag[:, E:] > 0, at_tail[:, E:], far)

    loads[3].wait()
    wait_received(0, tables)

    table = table_in[...].astype(BF)

    def slots(base, size, block, first, period):
        s = base + iota(size, D * FIELDS, 0)
        field_row = iota(size, D * FIELDS, 1)
        start = div(s, block) * FIELDS
        pick = jnp.where(field_row == start, 32.0, jnp.where(field_row == start + 1, 1.0, 0.0))
        lane = iota(size, 128, 1) == first + rem(base + iota(size, 128, 0), period)
        ids = jnp.sum(jnp.where(lane, dot(pick.astype(BF), table), 0.0), axis=1, keepdims=True)
        marks = jnp.sum(
            jnp.where(lane, dot(ones_where(field_row == start + 2), table), 0.0),
            axis=1, keepdims=True,
        )
        return ids - 32.0, marks

    chunk = min(512, D * tr)
    main_chunk = min(512, D * m)

    def answer_main(h):
        @pl.loop(0, D * m // main_chunk)
        def _(step):
            base = pl.multiple_of(step * main_chunk, main_chunk)
            ids, marks = slots(base, main_chunk, m, 0, m)
            if h == 1:
                main_row[:, pl.ds(base, main_chunk)] = to_row(ids).astype(I32)
                main_flag[:, pl.ds(base, main_chunk)] = to_row(marks)
            hit = ones_where(iota(main_chunk, N, 1) == ids.astype(I32))
            ans_main[h, pl.ds(base, main_chunk), :] = dot(
                hit, mem[:, h * HW : (h + 1) * HW]
            ).astype(BF)

        start_exchange(2 + h, ans_m[h])

    if m:
        answer_main(0)

    @pl.loop(0, D * tr // chunk)
    def _(step):
        base = pl.multiple_of(step * chunk, chunk)
        ids, marks = slots(base, chunk, tr, m, R)
        quarter = rem(div(base + iota(chunk, 1, 0), R), QUARTERS)
        tail_row[:, pl.ds(base, chunk)] = to_row(ids).astype(I32)
        tail_flag[:, pl.ds(base, chunk)] = to_row(jnp.where(quarter == 0, marks, 0.0))
        total = jnp.zeros((chunk, QW), F32)
        hit = ones_where(iota(chunk, N, 1) == ids.astype(I32))
        for q in range(QUARTERS):
            total = total + jnp.where(quarter == q, dot(hit, mem[:, q * QW : (q + 1) * QW]), 0.0)
        ans_tail[pl.ds(base, chunk), :] = total.astype(BF)

    start_exchange(1, ans_t)
    if m:
        answer_main(1)

    @pl.loop(0, N // TILE)
    def _(t):
        base = pl.multiple_of(t * TILE, TILE)
        nodes = base + iota(TILE, D * tr, 0)
        count = jnp.sum(jnp.where(tail_row[...] == nodes, tail_flag[...], 0.0), axis=1, keepdims=True)
        if m:
            nodes = base + iota(TILE, D * m, 0)
            count = count + jnp.sum(
                jnp.where(main_row[...] == nodes, main_flag[...], 0.0), axis=1, keepdims=True
            )
        tally[pl.ds(base, TILE), :] = count

    tally_row = to_row(tally[...])
    touched_row = jnp.where(tally_row > 0.5, 1.0, 0.0)
    earlier = ones_where(iota(N, N, 0) < iota(N, N, 1))
    before = dot(jnp.broadcast_to(touched_row, (8, N)).astype(BF), earlier)[0:1, :]
    rank_row = jnp.where(touched_row > 0.5, before, -1.0)
    rank_column = to_column(rank_row)
    rank[...] = jnp.broadcast_to(rank_column, (N, 128)).astype(I32)
    total_rows[...] = jnp.broadcast_to(
        jnp.sum(touched_row, axis=1, keepdims=True), (8, 128)
    ).astype(I32)

    def rank_slots(row_ref, count, size):
        @pl.loop(0, count // size)
        def _(step):
            cols = pl.ds(pl.multiple_of(step * size, size), size)
            same = iota(N, size, 0) == row_ref[:, cols]
            row_ref[:, cols] = jnp.sum(
                jnp.where(same, rank_column, 0.0), axis=0, keepdims=True
            ).astype(I32)

    rank_slots(tail_row, D * tr, chunk)
    if m:
        rank_slots(main_row, D * m, main_chunk)

    loads[4].wait()

    @pl.loop(0, ranks // TILE)
    def _(t):
        base = pl.multiple_of(t * TILE, TILE)
        rows = pl.ds(base, TILE)
        pick = rank_row.astype(I32) == base + iota(TILE, N, 0)
        tally[rows, :] = jnp.sum(jnp.where(pick, tally_row, 0.0), axis=1, keepdims=True)
        pick = ones_where(pick)

        @pl.loop(0, DM // TILE)
        def _(c):
            cols = pl.ds(pl.multiple_of(c * TILE, TILE), TILE)
            held[rows, cols] = dot(pick, mem[:, cols]).astype(BF)

    @pl.loop(0, 3 * DM // TILE)
    def _(t):
        cols = pl.ds(pl.multiple_of(t * TILE, TILE), TILE)
        gh[:, cols] = dot(held[...], wh[:, cols])

    stores = []
    for i, (src, dst) in enumerate(
        ((gh, gh_out), (held, held_out), (rank, rank_out), (total_rows, total_out))
    ):
        c = pltpu.make_async_copy(src, dst, store_sem.at[i])
        c.start()
        stores.append(c)

    for c in loads[5:10]:
        c.wait()
    feat_width = feat_ref.shape[1]

    @pl.loop(0, HID // TILE)
    def _(t):
        cols = pl.ds(pl.multiple_of(t * TILE, TILE), TILE)
        acc[:, cols] = dot(feat_ref[...], w1[2 * DM : 2 * DM + feat_width, cols]) + b1_ref[:, cols]

    quarter_row = rem(div(iota(1, D * tr, 1), R), QUARTERS)
    quarter_column = rem(div(iota(D * tr, 1, 0), R), QUARTERS)
    lane = iota(1, D * tr, 1) - quarter_row * R
    from_tail[...] = ones_where(jnp.broadcast_to(lane, (2 * E, D * tr)) == tail_column)
    if m:
        from_main = ones_where(iota(2 * E, D * m, 1) == main_column)

    @pl.loop(0, ranks // TILE)
    def _(t):
        base = pl.multiple_of(t * TILE, TILE)
        rows = pl.ds(base, TILE)
        sum_tail[rows, :] = ones_where(tail_row[...] == base + iota(TILE, D * tr, 0))
        if m:
            sum_main[rows, :] = ones_where(main_row[...] == base + iota(TILE, D * m, 0))

    def of_quarter(ref, q):
        return ref[...] * ones_where(quarter_column == q)

    for h in range(HALVES):
        wait_received(2 + h, ans_m[h])
        if h == 0:
            wait_received(1, ans_t)
        got = []
        for q in range(h * QUARTERS // HALVES, (h + 1) * QUARTERS // HALVES):
            got.append(dot(from_tail[...], of_quarter(ret_tail, q)))
        got = jnp.concatenate(got, axis=1)
        if m:
            got = got + dot(from_main, ret_main[h])
        fetched[...] = got.astype(BF)

        @pl.loop(0, HID // TILE)
        def _(t):
            cols = pl.ds(pl.multiple_of(t * TILE, TILE), TILE)
            total = acc[:, cols] + dot(fetched[0:E, :], w1[h * HW : (h + 1) * HW, cols])
            total = total + dot(fetched[E : 2 * E, :], w1[DM + h * HW : DM + (h + 1) * HW, cols])
            if h == HALVES - 1:
                hidden[:, cols] = jnp.maximum(total, 0.0).astype(BF)
            else:
                acc[:, cols] = total

    to_tail = ones_where(iota(D * tr, E, 0) - quarter_column * R == sent_tail)
    if m:
        to_main = ones_where(iota(D * m, E, 0) == sent_main)
    k = 2 + HALVES
    for h in range(HALVES):
        cols = slice(h * HW, (h + 1) * HW)
        message = (dot(hidden[...], w2[:, cols]) + b2_ref[:, cols]).astype(BF)
        if m:
            msg_main[h] = dot(to_main, message).astype(BF)
            start_exchange(k + 1 + h, msg_m[h])
        moved = dot(to_tail, message)
        for j in range(QUARTERS // HALVES):
            part = jnp.where(
                quarter_column == h * QUARTERS // HALVES + j, moved[:, j * QW : (j + 1) * QW], 0.0
            ).astype(BF)
            msg_tail[...] = part if h == 0 and j == 0 else msg_tail[...] + part

    start_exchange(k, msg_t)
    wait_sent(0, tables)
    wait_sent(1, ans_t)
    for h in range(HALVES):
        wait_sent(2 + h, ans_m[h])
    for c in stores:
        c.wait()

    loads[10].wait()
    loads[11].wait()

    for h in range(HALVES):
        wait_received(k + 1 + h, msg_m[h])
        if m:

            @pl.loop(0, ranks // TILE)
            def _(t):
                rows = pl.ds(pl.multiple_of(t * TILE, TILE), TILE)
                sums[rows, h * HW : (h + 1) * HW] = dot(sum_main[rows, :], inc_main[h])

    wait_received(k, msg_t)
    for q in range(QUARTERS):
        cols = slice(q * QW, (q + 1) * QW)
        part = of_quarter(inc_tail, q)
        for t in range(ranks // TILE):
            rows = slice(t * TILE, (t + 1) * TILE)
            summed = dot(sum_tail[rows, :], part)
            if m:
                summed = summed + sums[rows, cols]
            agg[rows, cols] = (summed / jnp.maximum(tally[rows, :], 1.0)).astype(BF)
    last = pltpu.make_async_copy(agg, agg_out, store_sem.at[4])
    last.start()

    copies = []
    for c in range(DM // TILE):
        cols = slice(c * TILE, (c + 1) * TILE)
        fresh[:, cols] = gru_columns(agg[0:TILE, :], wi, gb_ref, gh, held, c)
        copy = pltpu.make_async_copy(fresh.at[:, cols], fresh_out.at[:, cols], store_sem.at[5 + c])
        copy.start()
        copies.append(copy)
    last.wait()
    for copy in copies:
        copy.wait()
    wait_sent(k, msg_t)
    for h in range(HALVES):
        wait_sent(k + 1 + h, msg_m[h])


def gru_columns(agg, wi, gb, gh, held, c):
    DM = agg.shape[1]
    gates, hid = [], []
    for g in range(3):
        part = slice(g * DM + c * TILE, g * DM + (c + 1) * TILE)
        gates.append(dot(agg, wi[:, part]) + gb[:, part])
        hid.append(gh[0:TILE, part])
    reset = 0.5 * jnp.tanh(0.5 * (gates[0] + hid[0])) + 0.5
    update = 0.5 * jnp.tanh(0.5 * (gates[1] + hid[1])) + 0.5
    candidate = jnp.tanh(gates[2] + reset * hid[2])
    previous = held[0:TILE, c * TILE : (c + 1) * TILE].astype(F32)
    return ((1.0 - update) * candidate + update * previous).astype(BF)


def place_kernel(
    total_ref, rank_hbm, gb_hbm, mem_hbm, agg_hbm, held_hbm, wi_hbm, gh_hbm, fresh_hbm,
    out_hbm,
    rank_ref, gb_ref, mem, agg, held, wi, gh, fresh, out,
    first_sem, tile_sem, mem_sem, out_sem,
):
    N, DM = mem.shape
    steps = DM // TILE
    tiles = lax.div(total_ref[0, 0] + (TILE - 1), TILE)

    def columns(c):
        return slice(c * TILE, (c + 1) * TILE)

    def mem_copy(c):
        return pltpu.make_async_copy(
            mem_hbm.at[:, columns(c)], mem.at[:, columns(c)], mem_sem.at[c]
        )

    def out_copy(c):
        return pltpu.make_async_copy(
            out.at[:, columns(c)], out_hbm.at[:, columns(c)], out_sem.at[c]
        )

    def place(base, c, before):
        column = rank_ref[:, 0:1] - base
        moved = dot(ones_where(column == iota(N, TILE, 1)), fresh[:, columns(c)])
        mine = (column >= 0) & (column < TILE)
        out[:, columns(c)] = jnp.where(mine, moved, before[:, columns(c)].astype(F32)).astype(BF)

    starts = [
        pltpu.make_async_copy(rank_hbm, rank_ref, first_sem.at[0]),
        pltpu.make_async_copy(fresh_hbm, fresh, first_sem.at[1]),
    ]
    for c in starts:
        c.start()
    for c in range(steps):
        mem_copy(c).start()
    for c in starts:
        c.wait()
    for c in range(steps):
        mem_copy(c).wait()
        place(0, c, mem)

        @pl.when(tiles <= 1)
        def _():
            out_copy(c).start()

    @pl.loop(1, tiles)
    def _(t):
        base = pl.multiple_of(t * TILE, TILE)
        rows = pl.ds(base, TILE)
        pairs = (
            (agg_hbm.at[rows], agg), (held_hbm.at[rows], held), (gh_hbm.at[rows], gh),
            (wi_hbm, wi), (gb_hbm, gb_ref),
        )
        copies = [pltpu.make_async_copy(a, b, tile_sem.at[i]) for i, (a, b) in enumerate(pairs)]
        for copy in copies:
            copy.start()
        for copy in copies:
            copy.wait()
        for c in range(steps):
            fresh[:, columns(c)] = gru_columns(agg[...], wi, gb_ref, gh, held, c)
            place(base, c, out)

            @pl.when(t == tiles - 1)
            def _():
                out_copy(c).start()

    for c in range(steps):
        out_copy(c).wait()


def on_device(
    mesh_sizes,
    memory,
    ends_owner,
    ends_row,
    event_mask,
    edge_feat,
    msg_w1,
    msg_b1,
    msg_w2,
    msg_b2,
    gru_in,
    gru_hid,
    gru_bias,
):
    D, tm = mesh_sizes
    E = ends_owner.shape[0]
    N, DM = memory.shape
    HID = msg_w2.shape[0]
    cap = 5 * E // (2 * D)
    m = cap // 16 * 16
    R = max(4, -(-(cap - m) // 4) * 4)
    tr = QUARTERS * R
    QW = DM // QUARTERS
    mains = D * m if m else 16
    ranks = -(-min(N, D * cap) // TILE) * TILE
    smem = pl.BlockSpec(memory_space=pltpu.SMEM)
    hbm = pl.BlockSpec(memory_space=pltpu.HBM)
    phases = 3 + 2 * HALVES
    agg, gh, held, rank, total, fresh = pl.pallas_call(
        functools.partial(kernel, (D, tm, m, R)),
        out_shape=[
            jax.ShapeDtypeStruct((ranks, DM), BF),
            jax.ShapeDtypeStruct((ranks, 3 * DM), F32),
            jax.ShapeDtypeStruct((ranks, DM), BF),
            jax.ShapeDtypeStruct((N, 128), I32),
            jax.ShapeDtypeStruct((8, 128), I32),
            jax.ShapeDtypeStruct((TILE, DM), BF),
        ],
        in_specs=[hbm] * 12,
        out_specs=[hbm] * 6,
        scratch_shapes=[
            pltpu.VMEM((ranks, DM), BF),
            pltpu.VMEM((ranks, DM), BF),
            pltpu.VMEM((N, 128), I32),
            pltpu.VMEM((8, 128), I32),
            pltpu.VMEM((TILE, DM), BF),
            pltpu.VMEM(gru_in.shape, BF),
            pltpu.VMEM((1, 3 * DM), F32),
            pltpu.VMEM((2 * E, D * tr), BF),
            pltpu.VMEM((ranks if m else 16, mains), BF),
            pltpu.VMEM((ranks, D * tr), BF),
            pltpu.VMEM((2, E), I32),
            pltpu.VMEM((2, E), I32),
            pltpu.VMEM((1, E), I32),
            pltpu.VMEM(edge_feat.shape, BF),
            pltpu.VMEM((1, HID), F32),
            pltpu.VMEM((1, DM), F32),
            pltpu.VMEM(memory.shape, BF),
            pltpu.VMEM(msg_w1.shape, BF),
            pltpu.VMEM(msg_w2.shape, BF),
            pltpu.VMEM(gru_hid.shape, BF),
            pltpu.VMEM((ranks, 3 * DM), F32),
            pltpu.VMEM((D * FIELDS, 128), F32),
            pltpu.VMEM((D * FIELDS, 128), F32),
            pltpu.VMEM((2 * E, DM // HALVES), BF),
            pltpu.VMEM((E, HID), F32),
            pltpu.VMEM((E, HID), BF),
            pltpu.VMEM((N, 1), F32),
            pltpu.VMEM((1, mains), I32),
            pltpu.VMEM((1, mains), F32),
            pltpu.VMEM((1, D * tr), I32),
            pltpu.VMEM((1, D * tr), F32),
            pltpu.VMEM((ranks if m else 8, DM), F32),
        ]
        + [pltpu.VMEM((HALVES, mains, DM // HALVES), BF)] * 4
        + [pltpu.VMEM((D * tr, QW), BF)] * 4
        + [
            pltpu.SemaphoreType.DMA((12,)),
            pltpu.SemaphoreType.DMA((phases,)),
            pltpu.SemaphoreType.DMA((phases,)),
            pltpu.SemaphoreType.DMA((phases,)),
            pltpu.SemaphoreType.DMA((5 + DM // TILE,)),
        ],
        compiler_params=pltpu.CompilerParams(
            collective_id=0, has_side_effects=True, vmem_limit_bytes=60 * 2**20
        ),
    )(
        ends_owner.T,
        ends_row.T,
        event_mask.reshape(1, E),
        edge_feat,
        msg_b1.reshape(1, -1),
        msg_b2.reshape(1, -1),
        memory,
        msg_w1,
        msg_w2,
        gru_hid,
        gru_in,
        gru_bias.reshape(1, -1),
    )
    return pl.pallas_call(
        place_kernel,
        out_shape=jax.ShapeDtypeStruct((N, DM), BF),
        in_specs=[smem] + [hbm] * 8,
        out_specs=hbm,
        scratch_shapes=[
            pltpu.VMEM((N, 128), I32),
            pltpu.VMEM((1, 3 * DM), F32),
            pltpu.VMEM((N, DM), BF),
            pltpu.VMEM((TILE, DM), BF),
            pltpu.VMEM((TILE, DM), BF),
            pltpu.VMEM(gru_in.shape, BF),
            pltpu.VMEM((TILE, 3 * DM), F32),
            pltpu.VMEM((TILE, DM), BF),
            pltpu.VMEM((N, DM), BF),
            pltpu.SemaphoreType.DMA((2,)),
            pltpu.SemaphoreType.DMA((5,)),
            pltpu.SemaphoreType.DMA((DM // TILE,)),
            pltpu.SemaphoreType.DMA((DM // TILE,)),
        ],
        compiler_params=pltpu.CompilerParams(vmem_limit_bytes=60 * 2**20),
    )(total, rank, gru_bias.reshape(1, -1), memory, agg, held, gru_in, gh, fresh)


def solution(mesh):
    sizes = (mesh.shape["node"] * mesh.shape["tm"], mesh.shape["tm"])
    split = P(("node", "tm"))
    return jax.shard_map(
        functools.partial(on_device, sizes),
        mesh=mesh,
        in_specs=(split,) * 5 + (P(),) * 7,
        out_specs=split,
        check_vma=False,
    )
```
